512 devices in a mesh: tp: 16 (over z_lo, y), dp: 32 (over z_hi, x, core).
Axes of the slice: x: 4, y: 8, z: 8 (z_hi: 4, z_lo: 2; z = z_hi * 2 + z_lo), core: 2. Of those that a mesh axis runs over, the one named last changes fastest.
Arguments:
- tokens: bfloat16 [32, 2048, 5120], P('dp', None, 'tp'), may hold values from -6 to 6
- proximal_weight: bfloat16 [5120, 1024], P('tp'), may hold values from -0.078125 to 0.078125
- current_weight: bfloat16 [5120, 1024], P(('tp', 'dp')), may hold values from -0.078125 to 0.078125
- readout: bfloat16 [32, 2048, 1024], P('dp', 'tp'), may hold values from -0.0625 to 0.0625
- advantage: float32 [32, 2048], P('dp', 'tp'), may hold values from -5 to 5
- lengths: int32 [32, 8], P('dp'), may hold values from 1 to 1024, 2048 in all within a row
Outputs:
- grad_input: bfloat16 [32, 2048, 5120], P('dp', 'tp')
The draws below stay inside these ranges and needn't reach their ends.
Inputs may be any that keep to these rules, and one draw needn't show every extreme that they name: The lengths of each row sum to 2048; in every row the longest is exactly 1024.
All inputs are finite; a program needn't handle non-finite values.
Results may differ from the reference program's by a relative error of at most 0.0049.
Values may be sent and summed in bfloat16 or wider, within the bound.
A program may use at most 128 MiB of HBM per device.

```python
import math
import jax
import jax.numpy as jnp
import numpy as np
from jax import lax

MODEL_WIDTH = 5120
ROW_SEQUENCES = 8
KEY_FEATURE_COLS = 1024
ROW_TOKENS = 2048
PACKED_ROWS = 32
LONGEST_LENGTH = 1024


def block_scale(own_key, dims, split, least, high):
    def one(axis_at, blocks):
        heights = jax.random.uniform(jax.random.fold_in(jax.random.fold_in(own_key, 6), axis_at), (blocks,), jnp.float32, least / len(split), high / len(split))
        return jnp.repeat(jnp.exp(heights), dims[axis_at] // blocks).reshape((-1,) + (1,) * (len(dims) - axis_at - 1))

    level = one(*split[0])
    for cut in split[1:]:
        level = level * one(*cut)
    return level


def length_profile(number_of, total, bound, lean):
    loads = [(1 << 20) // math.isqrt(standing ** lean) + 1 for standing in range(2, number_of + 1)]
    rest, given = total - bound - (number_of - 1), [1] * (number_of - 1)
    while rest > 0:
        movable = [i for i in range(number_of - 1) if given[i] < bound]
        mass, left = sum([loads[i] for i in movable]), rest
        for i in movable:
            more = min(bound - given[i], max(1, left * loads[i] // mass), rest)
            given[i] = given[i] + more
            rest = rest - more
    return np.array([bound] + given)


def uneven_parts(own_key, number_of, total, reach, lean):
    if number_of == 2:
        one = jax.random.randint(own_key, (), max(1, total - reach), min(reach, total - 1) + 1)
        return jnp.stack([one, total - one])
    sizes = jnp.asarray(length_profile(number_of, total, reach, lean), jnp.int32)
    couples = (number_of - 1) // 2
    giver, taker = sizes[1:1 + 2 * couples:2], sizes[2:2 + 2 * couples:2]
    margin = jnp.minimum(giver - 1, reach - taker)
    passed = jax.random.randint(jax.random.fold_in(own_key, 1), (couples,), 0, 1 << 20) % (margin + 1)
    sizes = sizes.at[1:1 + 2 * couples:2].set(giver - passed).at[2:2 + 2 * couples:2].set(taker + passed)
    return sizes[jax.random.permutation(jax.random.fold_in(own_key, 2), number_of)]


def gaussian(key, shape, scale, limit, cuts=(), kind=jnp.bfloat16):
    values = scale * jax.random.normal(key, shape, jnp.float32)
    if cuts:
        values = values * block_scale(key, shape, cuts, -0.22, 0.18)
    return jnp.clip(values, -limit, limit).astype(kind)


def setup_inputs(seed: int = 0) -> dict:
    key_of = jax.random.split(jax.random.key(seed), 7)
    return {
        "tokens": gaussian(key_of[0], (PACKED_ROWS, ROW_TOKENS, MODEL_WIDTH), 1.0, 6.0, ((0, 32), (2, 16))),
        "proximal_weight": gaussian(key_of[1], (MODEL_WIDTH, KEY_FEATURE_COLS), MODEL_WIDTH ** -0.5, 0.078125, ((0, 16),)),
        "current_weight": gaussian(key_of[2], (MODEL_WIDTH, KEY_FEATURE_COLS), MODEL_WIDTH ** -0.5, 0.078125, ((0, 512),)),
        "readout": gaussian(key_of[3], (PACKED_ROWS, ROW_TOKENS, KEY_FEATURE_COLS), (8 * KEY_FEATURE_COLS) ** -0.5, 0.0625, ((0, 32), (1, 16))),
        "advantage": gaussian(key_of[4], (PACKED_ROWS, ROW_TOKENS), 1.0, 5.0, ((0, 32), (1, 16)), jnp.float32),
        "lengths": jax.vmap(lambda own: uneven_parts(own, ROW_SEQUENCES, ROW_TOKENS, LONGEST_LENGTH, 2))(jax.random.split(key_of[5], PACKED_ROWS)).reshape((PACKED_ROWS, ROW_SEQUENCES)).astype(jnp.int32),
    }


EPS_HIGH = 0.28
LOSS_MULTIPLIER = 64.0


def token_fractions(packed_row_lengths):
    seq_ends = jnp.cumsum(packed_row_lengths)
    seq_starts = seq_ends - packed_row_lengths
    token_positions = jnp.arange(ROW_TOKENS, dtype=jnp.int32)
    inside = (token_positions[None, :] >= seq_starts[:, None]) & (token_positions[None, :] < seq_ends[:, None])
    seq_share = 1.0 / (ROW_SEQUENCES * packed_row_lengths.astype(jnp.float32))
    return jnp.sum(jnp.where(inside, seq_share[:, None], jnp.float32(0.0)), axis=0)


def reference(tokens, proximal_weight, current_weight, readout, advantage, lengths):
    def one_row(packed):
        row_tokens, row_readout, row_advantage, packed_row_lengths = packed
        proximal_out = jnp.dot(row_tokens, proximal_weight, preferred_element_type=jnp.float32)
        current_out = jnp.dot(row_tokens, current_weight, preferred_element_type=jnp.float32)
        readout_f = row_readout.astype(jnp.float32)
        proximal_score = jnp.sum(proximal_out * readout_f, axis=1)
        current_score = jnp.sum(current_out * readout_f, axis=1)
        clipped_ratio = jnp.minimum(jnp.exp(current_score - proximal_score), 1.0 + EPS_HIGH)
        token_importance_weight = -LOSS_MULTIPLIER * ROW_TOKENS * token_fractions(packed_row_lengths) * clipped_ratio * row_advantage
        key_grad = (token_importance_weight[:, None] * readout_f).astype(jnp.bfloat16)
        result = lax.dot_general(key_grad, current_weight, (((1,), (1,)), ((), ())), preferred_element_type=jnp.float32)
        return result.astype(jnp.bfloat16)
    return lax.map(one_row, (tokens, readout, advantage, lengths))
```

```python
import jax
import jax.numpy as jnp
from jax import lax
from jax.experimental import pallas as pl
from jax.experimental.pallas import tpu as pltpu
from jax.sharding import PartitionSpec as P

EPS_HIGH = 0.28
LOSS_MULTIPLIER = 64.0
BF16, F32 = jnp.bfloat16, jnp.float32

NX, NY, NZ, NZH = 4, 8, 8, 4
OWN, FAR = 6, 7
TOK, SEG, COLS, SLICE, OUT = 128, 1024, 1024, 320, 5120
ROWS, PAD = 10, 16


def dot_nt(a, b):
    return lax.dot_general(a, b, (((1,), (1,)), ((), ())), preferred_element_type=F32)


def kernel(tok_hbm, wp_hbm, wc_ref, r_hbm, adv_ref, len_ref, out_ref,
           rb, tb, wpb, wg, wc, dw, gs, gb, ps, sb,
           loc, r_send, r_recv, wz_send, wz_recv, wx_send, wx_recv, ws_send, ws_recv,
           t_send, t_recv, g_send, g_recv, p_send, p_recv):
    tp, dp = lax.axis_index("tp"), lax.axis_index("dp")
    zl, y = lax.div(tp, NY), lax.rem(tp, NY)
    zh, x, core = lax.div(dp, 8), lax.rem(lax.div(dp, 2), NX), lax.rem(dp, 2)
    z = zh * 2 + zl

    def at(y_=None, x_=None, z_=None, core_=None):
        y_, x_ = y if y_ is None else y_, x if x_ is None else x_
        z_, core_ = z if z_ is None else z_, core if core_ is None else core_
        return {"tp": lax.rem(z_, 2) * NY + y_, "dp": lax.div(z_, 2) * 8 + x_ * 2 + core_}

    def ys(k):
        return lax.rem(y + (k + NY), NY)

    def xs(k):
        return lax.rem(x + (k + NX), NX)

    def zs(k):
        return lax.rem(z + (k + NZ), NZ)

    zpart = zh * 2 + (1 - zl)
    sibling = at(core_=1 - core)
    right, left = at(y_=ys(1)), at(y_=ys(-1))

    def remote(src, dst, send, recv, dev):
        return pltpu.make_async_remote_copy(src_ref=src, dst_ref=dst, send_sem=send, recv_sem=recv,
                                            device_id=dev, device_id_type=pl.DeviceIdType.MESH)

    barrier = pltpu.get_barrier_semaphore()
    peers = [at(y_=ys(k)) for k in range(1, NY)] + [at(z_=zs(k)) for k in range(1, NZ)]
    peers += [at(x_=xs(1)), at(x_=xs(-1)), sibling]
    for peer in peers:
        pl.semaphore_signal(barrier, inc=1, device_id=peer, device_id_type=pl.DeviceIdType.MESH)

    half = pl.ds(pl.multiple_of(zl * SEG, SEG), SEG)
    other = pl.ds(pl.multiple_of((1 - zl) * SEG, SEG), SEG)
    own_r = pltpu.make_async_copy(r_hbm, rb.at[OWN], loc.at[0])
    own_wp = pltpu.make_async_copy(wp_hbm, wpb.at[zl], loc.at[1])
    own_t = pltpu.make_async_copy(tok_hbm.at[:, half], tb.at[zl], loc.at[2])
    own_r.start()
    own_wp.start()
    own_t.start()
    mine = wg.at[zl, zh, x, core]
    mine[...] = jnp.zeros((PAD, COLS), BF16)
    mine[pl.ds(0, ROWS), :] = wc_ref[...]
    pl.semaphore_wait(barrier, len(peers))

    wz = {}
    for k in (1, 7, 2, 6, 3, 5, 4):
        wz[k] = remote(mine, mine, wz_send.at[k], wz_recv.at[k], at(z_=zs(k)))
        wz[k].start()

    def chunk(slot, h):
        return rb.at[slot, pl.ds(h * (TOK // 2), TOK // 2)]

    def slot_of(side, d):
        return OWN if d == 0 else FAR if d == 4 else 2 * (d - 1) + side

    def ring(side, d, h):
        i = 2 * d + h if d < 3 else 6
        return remote(chunk(slot_of(side, d), h), chunk(slot_of(side, d + 1), h),
                      r_send.at[side, i], r_recv.at[side, i], left if side else right)

    own_r.wait()
    rings = []
    for h in range(2):
        for side in range(2):
            c = ring(side, 0, h)
            c.start()
            rings.append(c)

    def forward(d, h):
        for side in range(2):
            ring(side, d - 1, h).wait_recv()
            if d < 3 or h == side:
                c = ring(side, d, h)
                c.start()
                rings.append(c)

    zp = at(z_=zpart)
    send_wp = remote(wp_hbm, wpb.at[zl], t_send.at[0], t_recv.at[0], zp)
    send_t = remote(tok_hbm.at[:, other], tb.at[zl], t_send.at[1], t_recv.at[1], zp)
    send_wp.start()
    send_t.start()

    forward(1, 0)
    forward(1, 1)

    def column(k):
        return wg.at[:, :, xs(k), core]

    for k in range(1, NZ):
        wz[k].wait_recv()
    wx, ws = [], []

    def share(k):
        c = remote(column(k), column(k), ws_send.at[k % NX], ws_recv.at[k % NX], sibling)
        c.start()
        ws.append(c)

    for i, k in enumerate((1, -1)):
        c = remote(column(0), column(0), wx_send.at[i], wx_recv.at[i], at(x_=xs(k)))
        c.start()
        wx.append(c)
    share(0)

    forward(2, 0)
    forward(2, 1)

    for i, k in enumerate((1, -1)):
        wx[i].wait_recv()
        part = wg.at[i, :, xs(-k), core]
        c = remote(part, part, wx_send.at[2 + i], wx_recv.at[2 + i], at(x_=xs(k)))
        c.start()
        wx.append(c)
        share(-k)

    forward(3, 0)
    forward(3, 1)

    wx[2].wait_recv()
    wx[3].wait_recv()
    share(2)
    for c in ws:
        c.wait_recv()

    r_i = lax.broadcasted_iota(jnp.int32, (SLICE, NZH * 8 * PAD), 0)
    q_i = lax.broadcasted_iota(jnp.int32, (SLICE, NZH * 8 * PAD), 1)
    q_r = q_i & (PAD - 1)
    pick = jnp.where((q_r < ROWS) & ((q_i >> 4) * ROWS + q_r == r_i), 1.0, 0.0).astype(BF16)
    for s in range(2):
        rows = wg[s].reshape(NZH * 8 * PAD, COLS)
        wc[pl.ds(s * SLICE, SLICE), :] = jnp.dot(pick, rows, preferred_element_type=F32).astype(BF16)

    gsend = []

    def send_g(slot, k):
        c = remote(gs.at[slot], gb.at[y], g_send.at[k], g_recv.at[k], at(y_=ys(k)))
        c.start()
        gsend.append(c)

    for d in range(1, 4):
        block = rb[2 * (d - 1):2 * d].reshape(2 * TOK, COLS)
        g = dot_nt(block, wc[...]).astype(BF16)
        gs[2 * (d - 1)] = g[:TOK]
        gs[2 * d - 1] = g[TOK:]
        send_g(2 * (d - 1), NY - d)
        send_g(2 * d - 1, d)
    ring(0, 3, 0).wait_recv()
    ring(1, 3, 1).wait_recv()
    g = dot_nt(rb[6:8].reshape(2 * TOK, COLS), wc[...]).astype(BF16)
    gs[FAR] = g[TOK:]
    send_g(FAR, 4)
    gb[y] = g[:TOK]

    own_wp.wait()
    send_wp.wait_recv()
    for s in range(2):
        dw[s] = (wc[pl.ds(s * SLICE, SLICE), :].astype(F32) - wpb[s].astype(F32)).astype(BF16)
    own_t.wait()
    send_t.wait_recv()
    shard_of = [-1, 1, -2, 2, -3, 3, 0, 4]
    psend = []
    for pair in range(4):
        block = rb[2 * pair:2 * pair + 2].reshape(2 * TOK, COLS)
        sums = [jnp.zeros((1, TOK), F32)] * 2
        for s in range(2):
            t = dot_nt(dw[s], block)
            for i in range(2):
                cols = pl.ds(pl.multiple_of(ys(shard_of[2 * pair + i]) * TOK, TOK), TOK)
                prod = t[:, i * TOK:(i + 1) * TOK] * tb[s, :, cols].astype(F32)
                sums[i] = sums[i] + jnp.sum(prod, axis=0, keepdims=True)
        for i in range(2):
            slot, k = 2 * pair + i, shard_of[2 * pair + i] % NY
            row = jnp.broadcast_to(sums[i], (8, TOK))
            if k == 0:
                sb[y] = row
            else:
                ps[slot] = row
                c = remote(ps.at[slot], sb.at[y], p_send.at[k], p_recv.at[k], at(y_=ys(k)))
                c.start()
                psend.append(c)

    pos = tp * TOK + lax.broadcasted_iota(jnp.int32, (8, TOK), 1)
    start = jnp.int32(0)
    shares = jnp.zeros((8, TOK), F32)
    for k in range(8):
        n = len_ref[0, k]
        inside = (pos >= start) & (pos < start + n)
        frac = 1.0 / (8.0 * jnp.broadcast_to(n, (8, TOK)).astype(F32))
        shares = shares + jnp.where(inside, frac, 0.0)
        start = start + n
    base = -LOSS_MULTIPLIER * 2048.0 * shares

    for c in psend:
        c.wait_recv()
    diff = jnp.sum(sb[...], axis=0)
    coef = base * jnp.minimum(jnp.exp(diff), 1.0 + EPS_HIGH) * adv_ref[...]
    coef = jnp.broadcast_to(coef[:1], (TOK, TOK))
    eye = (lax.broadcasted_iota(jnp.int32, (TOK, TOK), 0) == lax.broadcasted_iota(jnp.int32, (TOK, TOK), 1))
    scale = jnp.sum(jnp.where(eye, coef, 0.0), axis=1, keepdims=True)

    for c in gsend:
        c.wait_recv()
    for i in range(NY):
        g = gb[i].astype(F32) * scale
        for s in range(2):
            out_ref[:, (s * NY + i) * SLICE:(s * NY + i + 1) * SLICE] = g[:, s * SLICE:(s + 1) * SLICE].astype(BF16)

    for c in rings + list(wz.values()) + wx + ws + gsend + psend + [send_wp, send_t]:
        c.wait_send()


def local(tokens, proximal_weight, current_weight, readout, advantage, lengths):
    vmem, anywhere = pl.BlockSpec(memory_space=pltpu.VMEM), pl.BlockSpec(memory_space=pl.ANY)
    dma = pltpu.SemaphoreType.DMA
    out = pl.pallas_call(
        kernel,
        out_shape=jax.ShapeDtypeStruct((TOK, OUT), BF16),
        in_specs=[anywhere, anywhere, vmem, anywhere, vmem, pl.BlockSpec(memory_space=pltpu.SMEM)],
        out_specs=vmem,
        scratch_shapes=[
            pltpu.VMEM((8, TOK, COLS), BF16),
            pltpu.VMEM((2, SLICE, SEG), BF16),
            pltpu.VMEM((2, SLICE, COLS), BF16),
            pltpu.VMEM((2, NZH, NX, 2, PAD, COLS), BF16),
            pltpu.VMEM((2 * SLICE, COLS), BF16),
            pltpu.VMEM((2, SLICE, COLS), BF16),
            pltpu.VMEM((8, TOK, 2 * SLICE), BF16),
            pltpu.VMEM((8, TOK, 2 * SLICE), BF16),
            pltpu.VMEM((8, 8, TOK), F32),
            pltpu.VMEM((8, 8, TOK), F32),
            dma((3,)), dma((2, 7)), dma((2, 7)), dma((8,)), dma((8,)), dma((4,)), dma((4,)), dma((4,)), dma((4,)),
            dma((2,)), dma((2,)), dma((8,)), dma((8,)), dma((8,)), dma((8,)),
        ],
        compiler_params=pltpu.CompilerParams(
            collective_id=0, has_side_effects=True, vmem_limit_bytes=48 * 1024 * 1024),
        cost_estimate=pl.CostEstimate(flops=4 * 10**9, bytes_accessed=4 * 10**6, transcendentals=1024),
    )(jnp.swapaxes(tokens[0], 0, 1), proximal_weight, current_weight, readout[0], advantage, lengths)
    return out[None]


def solution(mesh):
    in_specs = (
        P("dp", None, "tp"),
        P("tp", None),
        P(("tp", "dp"), None),
        P("dp", "tp", None),
        P("dp", "tp"),
        P("dp", None),
    )
    return jax.shard_map(local, mesh=mesh, in_specs=in_specs, out_specs=P("dp", "tp", None), check_vma=False)
```

```python
import jax
import jax.numpy as jnp
from jax import lax
from jax.experimental import pallas as pl
from jax.experimental.pallas import tpu as pltpu
from jax.sharding import PartitionSpec as P

EPS_HIGH = 0.28
LOSS_MULTIPLIER = 64.0
BF16, F32 = jnp.bfloat16, jnp.float32

NX, NY, NZ, NZH = 4, 8, 8, 4
OWN, FAR = 6, 7
TOK, SEG, COLS, SLICE, OUT = 128, 1024, 1024, 320, 5120
ROWS, PAD = 10, 16
COL = NZ * ROWS
AWAY = (3, 4, 5)
FROWS = 32
FALL = NZH * NX * 2 * FROWS
VMEM_LIMIT = 60 * 1024 * 1024


def dot_nt(a, b):
    return lax.dot_general(a, b, (((1,), (1,)), ((), ())), preferred_element_type=F32)


def tenth(v):
    return (v * 6554) >> 16


def iota2(rows, cols):
    return lax.broadcasted_iota(jnp.int32, (rows, cols), 0), lax.broadcasted_iota(jnp.int32, (rows, cols), 1)


def one_where(mask):
    return jnp.where(mask, 1.0, 0.0).astype(BF16)


def kernel(tok_hbm, wp_hbm, wc_hbm, r_hbm, adv_hbm, len_hbm, out_ref,
           rb, tb, wpb, wz_b, wcol, wc, dw, jump, wfar, pick_far, gs, gb, ps, sb, wc_own, adv, lens,
           loc, r_send, r_recv, wz_send, wz_recv, wx_send, wx_recv, ws_send, ws_recv,
           t_send, t_recv, g_send, g_recv, p_send, p_recv,
           j_send, j_recv, fz_send, fz_recv, fx_send, fx_recv, fs_send, fs_recv):
    tp, dp = lax.axis_index("tp"), lax.axis_index("dp")
    zl, y = lax.div(tp, NY), lax.rem(tp, NY)
    zh, x, core = lax.div(dp, 8), lax.rem(lax.div(dp, 2), NX), lax.rem(dp, 2)
    z = zh * 2 + zl

    def at(y_=None, x_=None, z_=None, core_=None):
        y_, x_ = y if y_ is None else y_, x if x_ is None else x_
        z_, core_ = z if z_ is None else z_, core if core_ is None else core_
        return {"tp": lax.rem(z_, 2) * NY + y_, "dp": lax.div(z_, 2) * 8 + x_ * 2 + core_}

    def ys(k):
        return lax.rem(y + (k + NY), NY)

    def xs(k):
        return lax.rem(x + (k + NX), NX)

    def zs(k):
        return lax.rem(z + (k + NZ), NZ)

    sibling = at(core_=1 - core)
    right, left = at(y_=ys(1)), at(y_=ys(-1))
    up, down = at(z_=zs(1)), at(z_=zs(-1))
    started = []

    def remote(src, dst, send, recv, dev):
        return pltpu.make_async_remote_copy(src_ref=src, dst_ref=dst, send_sem=send, recv_sem=recv,
                                            device_id=dev, device_id_type=pl.DeviceIdType.MESH)

    def go(copy):
        copy.start()
        started.append(copy)
        return copy

    barrier = pltpu.get_barrier_semaphore()
    peers = [at(y_=ys(k)) for k in range(1, NY)] + [at(z_=zs(k)) for k in range(1, NZ)]
    peers += [at(x_=xs(1)), at(x_=xs(-1)), sibling]
    for peer in peers:
        pl.semaphore_signal(barrier, inc=1, device_id=peer, device_id_type=pl.DeviceIdType.MESH)

    half = pl.ds(pl.multiple_of(zl * SEG, SEG), SEG)
    other = pl.ds(pl.multiple_of((1 - zl) * SEG, SEG), SEG)
    loads = [pltpu.make_async_copy(src, dst, loc.at[i]) for i, (src, dst) in enumerate((
        (wc_hbm, wc_own), (r_hbm, rb.at[OWN]), (wp_hbm, wpb.at[zl]), (tok_hbm.at[:, half], tb.at[zl]),
        (adv_hbm, adv), (len_hbm, lens)))]
    for load in loads:
        load.start()
    mine = wz_b.at[z]
    mine[...] = jnp.zeros((PAD, COLS), BF16)
    loads[0].wait()
    mine[pl.ds(0, ROWS), :] = wc_own[...]
    loads[1].wait()
    pl.semaphore_wait(barrier, len(peers))

    wz = {}
    for k in (1, 7, 2, 6, 3, 5, 4):
        wz[k] = go(remote(mine, mine, wz_send.at[k], wz_recv.at[k], at(z_=zs(k))))
    jumps = [go(remote(mine, jump.at[i], j_send.at[i], j_recv.at[i], at(y_=ys(-k)))) for i, k in enumerate(AWAY)]

    def chunk(slot, h):
        return rb.at[slot, pl.ds(h * (TOK // 2), TOK // 2)]

    def slot_of(side, d):
        return OWN if d == 0 else FAR if d == 4 else 2 * (d - 1) + side

    def ring(side, d, h):
        i = 2 * d + h if d < 3 else 6
        return remote(chunk(slot_of(side, d), h), chunk(slot_of(side, d + 1), h),
                      r_send.at[side, i], r_recv.at[side, i], left if side else right)

    for h in range(2):
        for side in range(2):
            go(ring(side, 0, h))

    def forward(d):
        for h in range(2):
            for side in range(2):
                ring(side, d - 1, h).wait_recv()
                if d < 3 or h == side:
                    go(ring(side, d, h))

    def far_block(zz, part=None):
        ref = wfar.at[lax.rem(zz, 2), lax.div(zz, 2), x, core]
        return ref if part is None else ref.at[pl.ds(part * PAD, PAD)]

    def far_ring(side, d):
        block = far_block(zs(d if side else -d), side if d == 3 else None)
        return remote(block, block, fz_send.at[side, d], fz_recv.at[side, d], down if side else up)

    def far_came(side, d):
        block = far_block(zs((d + 1) if side else -(d + 1)), side if d == 3 else None)
        remote(block, block, fz_send.at[side, d], fz_recv.at[side, d], down if side else up).wait_recv()

    t_i, q_i = iota2(FROWS, 3 * PAD)
    pack = one_where((t_i < 3 * ROWS) & (tenth(t_i) * PAD + t_i - tenth(t_i) * ROWS == q_i))
    for c in jumps:
        c.wait_recv()
    wfar[zl, zh, x, core] = jnp.dot(
        pack, jump[...].reshape(3 * PAD, COLS), preferred_element_type=F32).astype(BF16)
    for side in range(2):
        go(far_ring(side, 0))

    zp = at(z_=zh * 2 + (1 - zl))
    wp_part = pl.ds(pl.multiple_of(core * (SLICE // 2), SLICE // 2), SLICE // 2)
    send_wp = go(remote(wp_hbm.at[wp_part], wpb.at[zl, wp_part], t_send.at[0], t_recv.at[0], zp))
    send_t = go(remote(tok_hbm.at[:, other], tb.at[zl], t_send.at[1], t_recv.at[1], zp))

    forward(1)
    for side in range(2):
        far_came(side, 0)
        go(far_ring(side, 1))

    t_i, q_i = iota2(COL, NZ * PAD)
    t_b = tenth(t_i)
    pick_col = one_where((2 * (t_b & (NZH - 1)) + (t_b >> 2)) * PAD + t_i - t_b * ROWS == q_i)
    for k in range(1, NZ):
        wz[k].wait_recv()
    wcol[x, core] = jnp.dot(
        pick_col, wz_b[...].reshape(NZ * PAD, COLS), preferred_element_type=F32).astype(BF16)

    def spread(buf, sends, recvs, sib_sends, sib_recvs, parts):
        def share(k):
            block = buf(xs(k), None)
            return go(remote(block, block, sib_sends.at[k % NX], sib_recvs.at[k % NX], sibling))

        own = [go(remote(buf(x, None), buf(x, None), sends.at[i], recvs.at[i], at(x_=xs(k))))
               for i, k in enumerate((1, -1))]
        shares = [share(0)]

        def second():
            for i, k in enumerate((1, -1)):
                own[i].wait_recv()
                block = buf(xs(-k), parts[i])
                own.append(go(remote(block, block, sends.at[2 + i], recvs.at[2 + i], at(x_=xs(k)))))
                shares.append(share(-k))

        def third():
            own[2].wait_recv()
            own[3].wait_recv()
            shares.append(share(2))

        def last():
            for c in shares:
                c.wait_recv()

        return second, third, last

    def near_buf(xx, part):
        ref = wcol.at[xx, core]
        return ref if part is None else ref.at[pl.ds(*part)]

    near = spread(near_buf, wx_send, wx_recv, ws_send, ws_recv, ((0, 48), (48, 32)))

    forward(2)
    for side in range(2):
        far_came(side, 1)
        go(far_ring(side, 2))
    near[0]()
    forward(3)
    for side in range(2):
        far_came(side, 2)
        go(far_ring(side, 3))
    near[1]()

    r_i, q_i = iota2(2 * SLICE, NX * 2 * COL)
    r_s = jnp.where(r_i >= SLICE, 1, 0)
    r_f = r_i - r_s * SLICE
    r_b = tenth(r_f)
    pick = one_where((r_b & 7) * COL + (r_s * NZH + (r_b >> 3)) * ROWS + r_f - r_b * ROWS == q_i)
    near[2]()
    wc[...] = jnp.dot(pick, wcol[...].reshape(NX * 2 * COL, COLS), preferred_element_type=F32).astype(BF16)

    gsend = []

    def send_g(slot, k):
        gsend.append(go(remote(gs.at[slot], gb.at[y], g_send.at[k], g_recv.at[k], at(y_=ys(k)))))

    for d in range(1, 3):
        block = rb[2 * (d - 1):2 * d].reshape(2 * TOK, COLS)
        g = dot_nt(block, wc[...]).astype(BF16)
        gs[2 * (d - 1)] = g[:TOK]
        gs[2 * d - 1] = g[TOK:]
        send_g(2 * (d - 1), NY - d)
        send_g(2 * d - 1, d)

    for side in range(2):
        far_came(side, 3)

    def far_buf(xx, part):
        return wfar.at[:, :, xx, core] if part is None else wfar.at[part, :, xx, core]

    far = spread(far_buf, fx_send, fx_recv, fs_send, fs_recv, (0, 1))

    ring(0, 3, 0).wait_recv()
    ring(1, 3, 1).wait_recv()
    loads[2].wait()
    send_wp.wait_recv()
    share_wp = go(remote(wpb.at[1 - zl, wp_part], wpb.at[1 - zl, wp_part], t_send.at[2], t_recv.at[2], sibling))
    gb[y] = dot_nt(rb[OWN], wc[...]).astype(BF16)

    q_i, f_i = iota2(FALL, SLICE)
    q_r = q_i & (FROWS - 1)
    for i in range(3):
        q_f = q_r - i * ROWS
        pick_far[i] = one_where((q_f >= 0) & (q_f < ROWS) & ((q_i >> 5) * ROWS + q_f == f_i))

    share_wp.wait_recv()
    for s in range(2):
        dw[s] = (wc[pl.ds(s * SLICE, SLICE), :].astype(F32) - wpb[s].astype(F32)).astype(BF16)
    loads[3].wait()
    send_t.wait_recv()
    far[0]()
    shard_of = [-1, 1, -2, 2, -3, 3, 0, 4]
    psend = []
    for pair in range(4):
        block = rb[2 * pair:2 * pair + 2].reshape(2 * TOK, COLS)
        sums = [jnp.zeros((1, TOK), F32)] * 2
        for s in range(2):
            t = dot_nt(dw[s], block)
            for i in range(2):
                cols = pl.ds(pl.multiple_of(ys(shard_of[2 * pair + i]) * TOK, TOK), TOK)
                prod = t[:, i * TOK:(i + 1) * TOK] * tb[s, :, cols].astype(F32)
                sums[i] = sums[i] + jnp.sum(prod, axis=0, keepdims=True)
        for i in range(2):
            slot, k = 2 * pair + i, shard_of[2 * pair + i] % NY
            row = jnp.broadcast_to(sums[i], (8, TOK))
            if k == 0:
                sb[y] = row
            else:
                ps[slot] = row
                psend.append(go(remote(ps.at[slot], sb.at[y], p_send.at[k], p_recv.at[k], at(y_=ys(k)))))

    loads[4].wait()
    loads[5].wait()
    pos = tp * TOK + lax.broadcasted_iota(jnp.int32, (8, TOK), 1)
    start = jnp.int32(0)
    shares = jnp.zeros((8, TOK), F32)
    for k in range(8):
        n = lens[0, k]
        inside = (pos >= start) & (pos < start + n)
        frac = 1.0 / (8.0 * jnp.broadcast_to(n, (8, TOK)).astype(F32))
        shares = shares + jnp.where(inside, frac, 0.0)
        start = start + n
    base = -LOSS_MULTIPLIER * 2048.0 * shares

    for c in psend:
        c.wait_recv()
    diff = jnp.sum(sb[...], axis=0)
    coef = base * jnp.minimum(jnp.exp(diff), 1.0 + EPS_HIGH) * adv[...]
    coef = jnp.broadcast_to(coef[:1], (TOK, TOK))
    t_i, q_i = iota2(TOK, TOK)
    scale = jnp.sum(jnp.where(t_i == q_i, coef, 0.0), axis=1, keepdims=True)

    far[1]()
    far[2]()
    for s in range(2):
        g = dot_nt(rb[OWN], wfar[s].reshape(FALL, COLS)).astype(BF16)
        for i, k in enumerate(AWAY):
            part = jnp.dot(g, pick_far[i], preferred_element_type=F32)
            gb[ys(k), :, s * SLICE:(s + 1) * SLICE] = part.astype(BF16)

    for c in gsend:
        c.wait_recv()
    for i in range(NY):
        g = gb[i].astype(F32) * scale
        for s in range(2):
            out_ref[:, (s * NY + i) * SLICE:(s * NY + i + 1) * SLICE] = g[:, s * SLICE:(s + 1) * SLICE].astype(BF16)

    for c in started:
        c.wait_send()


def local(tokens, proximal_weight, current_weight, readout, advantage, lengths):
    anywhere = pl.BlockSpec(memory_space=pl.ANY)
    dma, vmem = pltpu.SemaphoreType.DMA, pltpu.VMEM
    out = pl.pallas_call(
        kernel,
        out_shape=jax.ShapeDtypeStruct((TOK, OUT), BF16),
        in_specs=[anywhere] * 6,
        out_specs=pl.BlockSpec(memory_space=vmem),
        scratch_shapes=[
            vmem((8, TOK, COLS), BF16),
            vmem((2, SLICE, SEG), BF16),
            vmem((2, SLICE, COLS), BF16),
            vmem((NZ, PAD, COLS), BF16),
            vmem((NX, 2, COL, COLS), BF16),
            vmem((2 * SLICE, COLS), BF16),
            vmem((2, SLICE, COLS), BF16),
            vmem((3, PAD, COLS), BF16),
            vmem((2, NZH, NX, 2, FROWS, COLS), BF16),
            vmem((3, FALL, SLICE), BF16),
            vmem((4, TOK, 2 * SLICE), BF16),
            vmem((8, TOK, 2 * SLICE), BF16),
            vmem((8, 8, TOK), F32),
            vmem((8, 8, TOK), F32),
            vmem((ROWS, COLS), BF16),
            vmem((1, TOK), F32),
            pltpu.SMEM((1, 8), jnp.int32),
            dma((6,)), dma((2, 7)), dma((2, 7)), dma((8,)), dma((8,)), dma((4,)), dma((4,)), dma((4,)), dma((4,)),
            dma((3,)), dma((3,)), dma((8,)), dma((8,)), dma((8,)), dma((8,)),
            dma((3,)), dma((3,)), dma((2, 4)), dma((2, 4)), dma((4,)), dma((4,)), dma((4,)), dma((4,)),
        ],
        compiler_params=pltpu.CompilerParams(
            collective_id=0, has_side_effects=True, vmem_limit_bytes=VMEM_LIMIT),
        cost_estimate=pl.CostEstimate(flops=5 * 10**9, bytes_accessed=4 * 10**6, transcendentals=1024),
    )(jnp.swapaxes(tokens[0], 0, 1), proximal_weight, current_weight, readout[0], advantage, lengths)
    return out[None]


def solution(mesh):
    in_specs = (
        P("dp", None, "tp"),
        P("tp", None),
        P(("tp", "dp"), None),
        P("dp", "tp", None),
        P("dp", "tp"),
        P("dp", None),
    )
    return jax.shard_map(local, mesh=mesh, in_specs=in_specs, out_specs=P("dp", "tp", None), check_vma=False)
```

```python
import jax
import jax.numpy as jnp
from jax import lax
from jax.experimental import pallas as pl
from jax.experimental.pallas import tpu as pltpu
from jax.sharding import PartitionSpec as P

EPS_HIGH = 0.28
LOSS_MULTIPLIER = 64.0
BF16, F32 = jnp.bfloat16, jnp.float32

NX, NY, NZ, NZH = 4, 8, 8, 4
OWN, FAR = 6, 7
TOK, SEG, COLS, SLICE, OUT = 128, 1024, 1024, 320, 5120
ROWS, PAD = 10, 16
COL = NZ * ROWS
VMEM_LIMIT = 60 * 1024 * 1024


def dot_nt(a, b):
    return lax.dot_general(a, b, (((1,), (1,)), ((), ())), preferred_element_type=F32)


def tenth(v):
    return (v * 6554) >> 16


def rows_of(n):
    return lax.broadcasted_iota(jnp.int32, (n, 1), 0)


def ones_at(column, cols):
    shape = (column.shape[0], cols)
    at = jnp.broadcast_to(column, shape) == lax.broadcasted_iota(jnp.int32, shape, 1)
    return jnp.where(at, 1.0, 0.0).astype(BF16)


def kernel(tok_hbm, wp_hbm, wc_hbm, r_hbm, adv_hbm, len_hbm, out_ref,
           rb, tb, wpb, wz_b, wcol, wc, dw, pick, gs, gb, ps, sb, wc_own, adv, lens,
           loc, r_send, r_recv, wz_send, wz_recv, wx_send, wx_recv, ws_send, ws_recv,
           t_send, t_recv, g_send, g_recv, p_send, p_recv, j_send, j_recv):
    tp, dp = lax.axis_index("tp"), lax.axis_index("dp")
    zl, y = lax.div(tp, NY), lax.rem(tp, NY)
    zh, x, core = lax.div(dp, 8), lax.rem(lax.div(dp, 2), NX), lax.rem(dp, 2)
    z = zh * 2 + zl

    def at(y_=None, x_=None, z_=None, core_=None):
        y_, x_ = y if y_ is None else y_, x if x_ is None else x_
        z_, core_ = z if z_ is None else z_, core if core_ is None else core_
        return {"tp": lax.rem(z_, 2) * NY + y_, "dp": lax.div(z_, 2) * 8 + x_ * 2 + core_}

    def ys(k):
        return lax.rem(y + (k + NY), NY)

    def xs(k):
        return lax.rem(x + (k + NX), NX)

    sibling = at(core_=1 - core)
    right, left = at(y_=ys(1)), at(y_=ys(-1))
    partner = at(z_=zh * 2 + (1 - zl))
    started = []

    def remote(src, dst, send, recv, dev):
        return pltpu.make_async_remote_copy(src_ref=src, dst_ref=dst, send_sem=send, recv_sem=recv,
                                            device_id=dev, device_id_type=pl.DeviceIdType.MESH)

    def go(copy):
        copy.start()
        started.append(copy)
        return copy

    barrier = pltpu.get_barrier_semaphore()
    peers = [at(y_=ys(k)) for k in range(1, NY)] + [at(x_=xs(1)), at(x_=xs(-1)), sibling]

    def greet(peer):
        pl.semaphore_signal(barrier, inc=1, device_id=peer, device_id_type=pl.DeviceIdType.MESH)

    for peer in peers:
        greet(peer)
    for j in range(NZ):
        @pl.when(z < j)
        def _():
            greet(at(z_=j))

    half = pl.ds(pl.multiple_of(zl * SEG, SEG), SEG)
    other = pl.ds(pl.multiple_of((1 - zl) * SEG, SEG), SEG)
    loads = [pltpu.make_async_copy(src, dst, loc.at[i]) for i, (src, dst) in enumerate((
        (wc_hbm, wc_own), (r_hbm, rb.at[OWN]), (wp_hbm, wpb.at[zl]), (tok_hbm.at[:, half], tb.at[zl]),
        (adv_hbm, adv), (len_hbm, lens)))]
    for load in loads:
        load.start()
    mine = wz_b.at[0, z]
    mine[...] = jnp.zeros((PAD, COLS), BF16)
    loads[0].wait()
    mine[pl.ds(0, ROWS), :] = wc_own[...]
    loads[1].wait()
    pl.semaphore_wait(barrier, len(peers) + z)

    def give(w, to):
        block = wz_b.at[w, z]
        return remote(block, block, wz_send.at[w, to], wz_recv.at[w, z], at(z_=to))

    def came(w, b):
        block = wz_b.at[w, b]
        remote(block, block, wz_send.at[w, b], wz_recv.at[w, b], sibling).wait_recv()

    def lower(w):
        for k in range(1, NZ):
            @pl.when(k <= z)
            def _():
                give(w, z - k).start()

    def higher(w, *steps):
        for k in steps:
            @pl.when(z + k < NZ)
            def _():
                if w == 0:
                    came(w, z + k)
                give(w, z + k).start()

    def gathered(w):
        for b in range(NZ):
            @pl.when((b < z) if w == 0 else (b != z))
            def _():
                came(w, b)

    def settle(w):
        for b in range(NZ):
            @pl.when(b != z)
            def _():
                give(w, b).wait_send()

    lower(0)

    def chunk(slot, h):
        return rb.at[slot, pl.ds(h * (TOK // 2), TOK // 2)]

    def slot_of(side, d):
        return OWN if d == 0 else FAR if d == 4 else 2 * (d - 1) + side

    def ring(side, d, h):
        i = 2 * d + h if d < 3 else 6
        return remote(chunk(slot_of(side, d), h), chunk(slot_of(side, d + 1), h),
                      r_send.at[side, i], r_recv.at[side, i], left if side else right)

    go(ring(0, 0, 0))
    go(ring(1, 0, 0))
    jump = go(remote(mine, wz_b.at[1, z], j_send, j_recv, at(y_=ys(4))))
    go(ring(0, 0, 1))
    go(ring(1, 0, 1))

    def forward(d, h):
        for side in range(2):
            ring(side, d - 1, h).wait_recv()
            if d < 3 or h == side:
                go(ring(side, d, h))

    t_i = rows_of(COL)
    t_b = tenth(t_i)
    pick_col = ones_at((2 * (t_b & (NZH - 1)) + (t_b >> 2)) * PAD + t_i - t_b * ROWS, NZ * PAD)
    r_i = rows_of(2 * SLICE)
    r_s = jnp.where(r_i >= SLICE, 1, 0)
    r_f = r_i - r_s * SLICE
    r_b = tenth(r_f)
    pick[...] = ones_at((r_b & 7) * COL + (r_s * NZH + (r_b >> 3)) * ROWS + r_f - r_b * ROWS, NX * 2 * COL)

    higher(0, 1, 2)
    forward(1, 0)
    higher(0, 3, 4)
    forward(1, 1)
    higher(0, 5, 6, 7)
    jump.wait_recv()

    def spread(w):
        def block(k, part=None):
            ref = wcol.at[w, xs(k), core]
            return ref if part is None else ref.at[pl.ds(*part)]

        def over(i, k, src):
            return go(remote(src, src, wx_send.at[w, i], wx_recv.at[w, i], at(x_=xs(k))))

        def share(k):
            shares.append(go(remote(block(k), block(k), ws_send.at[w, k % NX], ws_recv.at[w, k % NX], sibling)))

        own, shares = [], []

        def first():
            gathered(w)
            wcol[w, x, core] = jnp.dot(
                pick_col, wz_b[w].reshape(NZ * PAD, COLS), preferred_element_type=F32).astype(BF16)
            own.extend(over(i, k, block(0)) for i, k in enumerate((1, -1)))
            share(0)

        def second():
            for i, (k, part) in enumerate(((1, (0, 48)), (-1, (48, 32)))):
                own[i].wait_recv()
                own.append(over(2 + i, k, block(-k, part)))
                share(-k)

        def third():
            own[2].wait_recv()
            own[3].wait_recv()
            share(2)

        def last():
            for c in shares:
                c.wait_recv()
            wc[w] = jnp.dot(
                pick[...], wcol[w].reshape(NX * 2 * COL, COLS), preferred_element_type=F32).astype(BF16)

        return first, second, third, last

    near, far = spread(0), spread(1)
    near[0]()
    forward(2, 0)
    lower(1)
    higher(1, *range(1, NZ))
    wp_part = pl.ds(pl.multiple_of(core * (SLICE // 2), SLICE // 2), SLICE // 2)
    send_wp = go(remote(wp_hbm.at[wp_part], wpb.at[zl, wp_part], t_send.at[0], t_recv.at[0], partner))
    send_t = go(remote(tok_hbm.at[:, other], tb.at[zl], t_send.at[1], t_recv.at[1], partner))
    forward(2, 1)
    near[1]()
    forward(3, 0)
    near[2]()
    near[3]()

    gsend = []

    def send_g(slot, k):
        gsend.append(go(remote(gs.at[slot], gb.at[y], g_send.at[k], g_recv.at[k], at(y_=ys(k)))))

    def gradient(d):
        block = rb[2 * (d - 1):2 * d].reshape(2 * TOK, COLS)
        g = dot_nt(block, wc[0]).astype(BF16)
        gs[2 * (d - 1)] = g[:TOK]
        gs[2 * d - 1] = g[TOK:]
        send_g(2 * (d - 1), NY - d)
        send_g(2 * d - 1, d)

    gradient(1)
    forward(3, 1)
    gradient(2)
    gradient(3)
    far[0]()
    loads[2].wait()
    send_wp.wait_recv()
    share_wp = go(remote(wpb.at[1 - zl, wp_part], wpb.at[1 - zl, wp_part], t_send.at[2], t_recv.at[2], sibling))

    share_wp.wait_recv()
    for s in range(2):
        dw[s] = (wc[0, pl.ds(s * SLICE, SLICE), :].astype(F32) - wpb[s].astype(F32)).astype(BF16)
    ring(0, 3, 0).wait_recv()
    ring(1, 3, 1).wait_recv()
    shard_of = [-1, 1, -2, 2, -3, 3, 0, 4]

    def scores(s, pair):
        t = dot_nt(dw[s], rb[2 * pair:2 * pair + 2].reshape(2 * TOK, COLS))
        sums = []
        for i in range(2):
            cols = pl.ds(pl.multiple_of(ys(shard_of[2 * pair + i]) * TOK, TOK), TOK)
            prod = t[:, i * TOK:(i + 1) * TOK] * tb[s, :, cols].astype(F32)
            sums.append(jnp.sum(prod, axis=0, keepdims=True))
        return sums

    loads[3].wait()
    first = [scores(zl, pair) for pair in range(4)]
    gb[y] = dot_nt(rb[OWN], wc[0]).astype(BF16)
    far[1]()
    send_t.wait_recv()
    psend = []
    for pair in range(4):
        second = scores(1 - zl, pair)
        for i in range(2):
            slot, k = 2 * pair + i, shard_of[2 * pair + i] % NY
            row = jnp.broadcast_to(first[pair][i] + second[i], (8, TOK))
            if k == 0:
                sb[y] = row
            else:
                ps[slot] = row
                psend.append(go(remote(ps.at[slot], sb.at[y], p_send.at[k], p_recv.at[k], at(y_=ys(k)))))

    loads[4].wait()
    loads[5].wait()
    pos = tp * TOK + lax.broadcasted_iota(jnp.int32, (8, TOK), 1)
    start = jnp.int32(0)
    shares = jnp.zeros((8, TOK), F32)
    for k in range(8):
        n = lens[0, k]
        inside = (pos >= start) & (pos < start + n)
        frac = 1.0 / (8.0 * jnp.broadcast_to(n, (8, TOK)).astype(F32))
        shares = shares + jnp.where(inside, frac, 0.0)
        start = start + n
    base = -LOSS_MULTIPLIER * 2048.0 * shares

    far[2]()
    far[3]()
    gb[ys(4)] = dot_nt(rb[OWN], wc[1]).astype(BF16)

    for c in psend:
        c.wait_recv()
    diff = jnp.sum(sb[...], axis=0)
    coef = base * jnp.minimum(jnp.exp(diff), 1.0 + EPS_HIGH) * adv[...]
    coef = jnp.broadcast_to(coef[:1], (TOK, TOK))
    eye = ones_at(rows_of(TOK), TOK).astype(F32)
    scale = jnp.sum(jnp.where(eye > 0.0, coef, 0.0), axis=1, keepdims=True)

    for c in gsend:
        c.wait_recv()
    for i in range(NY):
        g = gb[i].astype(F32) * scale
        for s in range(2):
            out_ref[:, (s * NY + i) * SLICE:(s * NY + i + 1) * SLICE] = g[:, s * SLICE:(s + 1) * SLICE].astype(BF16)

    for c in started:
        c.wait_send()
    settle(0)
    settle(1)


def local(tokens, proximal_weight, current_weight, readout, advantage, lengths):
    anywhere = pl.BlockSpec(memory_space=pl.ANY)
    dma, vmem = pltpu.SemaphoreType.DMA, pltpu.VMEM
    out = pl.pallas_call(
        kernel,
        out_shape=jax.ShapeDtypeStruct((TOK, OUT), BF16),
        in_specs=[anywhere] * 6,
        out_specs=pl.BlockSpec(memory_space=vmem),
        scratch_shapes=[
            vmem((8, TOK, COLS), BF16),
            vmem((2, SLICE, SEG), BF16),
            vmem((2, SLICE, COLS), BF16),
            vmem((2, NZ, PAD, COLS), BF16),
            vmem((2, NX, 2, COL, COLS), BF16),
            vmem((2, 2 * SLICE, COLS), BF16),
            vmem((2, SLICE, COLS), BF16),
            vmem((2 * SLICE, NX * 2 * COL), BF16),
            vmem((6, TOK, 2 * SLICE), BF16),
            vmem((8, TOK, 2 * SLICE), BF16),
            vmem((8, 8, TOK), F32),
            vmem((8, 8, TOK), F32),
            vmem((ROWS, COLS), BF16),
            vmem((1, TOK), F32),
            pltpu.SMEM((1, 8), jnp.int32),
            dma((6,)), dma((2, 7)), dma((2, 7)), dma((2, 8)), dma((2, 8)),
            dma((2, 4)), dma((2, 4)), dma((2, 4)), dma((2, 4)),
            dma((3,)), dma((3,)), dma((8,)), dma((8,)), dma((8,)), dma((8,)), dma, dma,
        ],
        compiler_params=pltpu.CompilerParams(
            collective_id=0, has_side_effects=True, vmem_limit_bytes=VMEM_LIMIT),
        cost_estimate=pl.CostEstimate(flops=5 * 10**9, bytes_accessed=4 * 10**6, transcendentals=1024),
    )(jnp.swapaxes(tokens[0], 0, 1), proximal_weight, current_weight, readout[0], advantage, lengths)
    return out[None]


def solution(mesh):
    in_specs = (
        P("dp", None, "tp"),
        P("tp", None),
        P(("tp", "dp"), None),
        P("dp", "tp", None),
        P("dp", "tp"),
        P("dp", None),
    )
    return jax.shard_map(local, mesh=mesh, in_specs=in_specs, out_specs=P("dp", "tp", None), check_vma=False)
```

```python
import jax
import jax.numpy as jnp
from jax import lax
from jax.experimental import pallas as pl
from jax.experimental.pallas import tpu as pltpu
from jax.sharding import PartitionSpec as P

EPS_HIGH = 0.28
LOSS_MULTIPLIER = 64.0
BF16, F32 = jnp.bfloat16, jnp.float32

NX, NY, NZ, NZH = 4, 8, 8, 4
OWN, FAR = 6, 7
TOK, SEG, COLS, SLICE, OUT = 128, 1024, 1024, 320, 5120
ROWS, PAD = 10, 16
COL = NZ * ROWS
VMEM_LIMIT = 60 * 1024 * 1024


def dot_nt(a, b):
    return lax.dot_general(a, b, (((1,), (1,)), ((), ())), preferred_element_type=F32)


def tenth(v):
    return (v * 6554) >> 16


def rows_of(n):
    return lax.broadcasted_iota(jnp.int32, (n, 1), 0)


def ones_at(column, cols):
    shape = (column.shape[0], cols)
    at = jnp.broadcast_to(column, shape) == lax.broadcasted_iota(jnp.int32, shape, 1)
    return jnp.where(at, 1.0, 0.0).astype(BF16)


def kernel(tok_hbm, wp_hbm, wc_hbm, r_hbm, adv_hbm, len_hbm, out_ref,
           rb, tb, wpb, wg, wz_b, wcol, wc, dw, pick, pick_near, gs, gb, ps, sb, wc_own, adv, lens,
           loc, r_send, r_recv, wz_send, wz_recv, wx_send, wx_recv, ws_send, ws_recv, nx_send, nx_recv, ny_send, ny_recv, ns_send, ns_recv,
           t_send, t_recv, g_send, g_recv, p_send, p_recv, j_send, j_recv):
    tp, dp = lax.axis_index("tp"), lax.axis_index("dp")
    zl, y = lax.div(tp, NY), lax.rem(tp, NY)
    zh, x, core = lax.div(dp, 8), lax.rem(lax.div(dp, 2), NX), lax.rem(dp, 2)
    z = zh * 2 + zl

    def at(y_=None, x_=None, z_=None, core_=None):
        y_, x_ = y if y_ is None else y_, x if x_ is None else x_
        z_, core_ = z if z_ is None else z_, core if core_ is None else core_
        return {"tp": lax.rem(z_, 2) * NY + y_, "dp": lax.div(z_, 2) * 8 + x_ * 2 + core_}

    def ys(k):
        return lax.rem(y + (k + NY), NY)

    def xs(k):
        return lax.rem(x + (k + NX), NX)

    sibling = at(core_=1 - core)
    right, left = at(y_=ys(1)), at(y_=ys(-1))
    partner = at(z_=zh * 2 + (1 - zl))
    started = []

    def remote(src, dst, send, recv, dev):
        return pltpu.make_async_remote_copy(src_ref=src, dst_ref=dst, send_sem=send, recv_sem=recv,
                                            device_id=dev, device_id_type=pl.DeviceIdType.MESH)

    def go(copy):
        copy.start()
        started.append(copy)
        return copy

    barrier = pltpu.get_barrier_semaphore()
    peers = [at(y_=ys(k)) for k in range(1, NY)] + [at(x_=xs(1)), at(x_=xs(-1)), sibling]

    def greet(peer):
        pl.semaphore_signal(barrier, inc=1, device_id=peer, device_id_type=pl.DeviceIdType.MESH)

    for peer in peers:
        greet(peer)
    for j in range(NZ):
        @pl.when(z < j)
        def _():
            greet(at(z_=j))

    half = pl.ds(pl.multiple_of(zl * SEG, SEG), SEG)
    other = pl.ds(pl.multiple_of((1 - zl) * SEG, SEG), SEG)
    loads = [pltpu.make_async_copy(src, dst, loc.at[i]) for i, (src, dst) in enumerate((
        (wc_hbm, wc_own), (r_hbm, rb.at[OWN]), (wp_hbm, wpb.at[zl]), (tok_hbm.at[:, half], tb.at[zl]),
        (adv_hbm, adv), (len_hbm, lens)))]
    for load in loads:
        load.start()
    mine = wg.at[zl, zh, x, core]
    mine[...] = jnp.zeros((PAD, COLS), BF16)
    loads[0].wait()
    mine[pl.ds(0, ROWS), :] = wc_own[...]
    loads[1].wait()
    pl.semaphore_wait(barrier, len(peers) + z)

    def block(w, b):
        return wz_b.at[b] if w else wg.at[lax.rem(b, 2), lax.div(b, 2), x, core]

    def give(w, to):
        return remote(block(w, z), block(w, z), wz_send.at[w, to], wz_recv.at[w, z], at(z_=to))

    def came(w, b):
        remote(block(w, b), block(w, b), wz_send.at[w, b], wz_recv.at[w, b], sibling).wait_recv()

    def near_block(b, k):
        return wg.at[lax.rem(b, 2), lax.div(b, 2), xs(k), core]

    def near_over(b, i):
        src = near_block(b, 0)
        return remote(src, src, nx_send.at[i, b], nx_recv.at[i, b], at(x_=xs(-1 if i else 1)))

    def near_on(b, i):
        src = near_block(b, 1 if i else -1)
        return remote(src, src, ny_send.at[b], ny_recv.at[b], at(x_=xs(-1 if i else 1)))

    def over(b):
        for i in range(2):
            near_over(b, i).start()

    def lower():
        for k in range(1, NZ):
            @pl.when(k <= z)
            def _():
                give(0, z - k).start()

    def higher(*steps):
        for k in steps:
            @pl.when(z + k < NZ)
            def _():
                came(0, z + k)
                give(0, z + k).start()
                over(z + k)

    def from_lower():
        for k in range(1, NZ):
            @pl.when(k <= z)
            def _():
                came(0, z - k)
                over(z - k)

    def onward(b):
        for i in range(2):
            src = near_block(b, 1 if i else -1)
            remote(src, src, nx_send.at[i, b], nx_recv.at[i, b], sibling).wait_recv()
        for i in range(2):
            @pl.when(lax.rem(b, 2) == i)
            def _():
                near_on(b, i).start()

    def onward_lower():
        for k in range(NZ):
            @pl.when(k <= z)
            def _():
                onward(z - k)

    def onward_higher():
        for k in range(1, NZ):
            @pl.when(z + k < NZ)
            def _():
                onward(z + k)

    def near_column(k):
        return wg.at[:, :, xs(k), core]

    def near_share(k):
        c = remote(near_column(k), near_column(k), ns_send.at[k % NX], ns_recv.at[k % NX], sibling)
        return go(c)

    def gathered():
        for b in range(NZ):
            @pl.when(b != z)
            def _():
                came(1, b)

    def settle():
        for b in range(NZ):
            @pl.when(b != z)
            def _():
                give(0, b).wait_send()
            for i in range(2):
                near_over(b, i).wait_send()
            near_on(b, b % 2).wait_send()

    lower()
    over(z)

    def chunk(slot, h):
        return rb.at[slot, pl.ds(h * (TOK // 2), TOK // 2)]

    def slot_of(side, d):
        return OWN if d == 0 else FAR if d == 4 else 2 * (d - 1) + side

    def ring(side, d, h):
        i = 2 * d + h if d < 3 else 6
        return remote(chunk(slot_of(side, d), h), chunk(slot_of(side, d + 1), h),
                      r_send.at[side, i], r_recv.at[side, i], left if side else right)

    go(ring(0, 0, 0))
    go(ring(1, 0, 0))
    jump = go(remote(mine, wz_b.at[z], j_send, j_recv, at(y_=ys(4))))
    go(ring(0, 0, 1))
    go(ring(1, 0, 1))

    def forward(d, h):
        for side in range(2):
            ring(side, d - 1, h).wait_recv()
            if d < 3 or h == side:
                go(ring(side, d, h))

    t_i = rows_of(COL)
    t_b = tenth(t_i)
    pick_col = ones_at((2 * (t_b & (NZH - 1)) + (t_b >> 2)) * PAD + t_i - t_b * ROWS, NZ * PAD)
    r_i = rows_of(2 * SLICE)
    r_s = jnp.where(r_i >= SLICE, 1, 0)
    r_f = r_i - r_s * SLICE
    r_b = tenth(r_f)
    q_i = rows_of(SLICE)
    q_b = tenth(q_i)
    pick_near[...] = ones_at(q_b * PAD + q_i - q_b * ROWS, NZH * 8 * PAD)
    pick[...] = ones_at((r_b & 7) * COL + (r_s * NZH + (r_b >> 3)) * ROWS + r_f - r_b * ROWS, NX * 2 * COL)

    forward(1, 0)
    higher(1, 2, 3, 4)
    from_lower()
    higher(5, 6, 7)
    jump.wait_recv()
    for k in range(1, NZ):
        go(give(1, lax.rem(z + k, NZ)))
    onward_lower()
    forward(1, 1)
    shares = [near_share(0)]
    onward_higher()
    shares += [near_share(1), near_share(-1)]
    forward(2, 0)

    def column(k, part=None):
        ref = wcol.at[xs(k), core]
        return ref if part is None else ref.at[pl.ds(*part)]

    def far_over(i, k, src):
        return go(remote(src, src, wx_send.at[i], wx_recv.at[i], at(x_=xs(k))))

    far_own, far_shares = [], []

    def far_share(k):
        far_shares.append(go(remote(column(k), column(k), ws_send.at[k % NX], ws_recv.at[k % NX], sibling)))

    def far_first():
        gathered()
        wcol[x, core] = jnp.dot(
            pick_col, wz_b[...].reshape(NZ * PAD, COLS), preferred_element_type=F32).astype(BF16)
        far_own.extend(far_over(i, k, column(0)) for i, k in enumerate((1, -1)))
        far_share(0)

    def far_second():
        for i, (k, part) in enumerate(((1, (0, 48)), (-1, (48, 32)))):
            far_own[i].wait_recv()
            far_own.append(far_over(2 + i, k, column(-k, part)))
            far_share(-k)

    def far_third():
        far_own[2].wait_recv()
        far_own[3].wait_recv()
        far_share(2)

    def far_last():
        for c in far_shares:
            c.wait_recv()
        wc[1] = jnp.dot(
            pick[...], wcol[...].reshape(NX * 2 * COL, COLS), preferred_element_type=F32).astype(BF16)

    for b in range(NZ):
        near_on(b, b % 2).wait_recv()
    shares.append(near_share(2))
    send_t = go(remote(tok_hbm.at[:, other], tb.at[zl], t_send.at[1], t_recv.at[1], partner))
    wp_part = pl.ds(pl.multiple_of(core * (SLICE // 2), SLICE // 2), SLICE // 2)
    send_wp = go(remote(wp_hbm.at[wp_part], wpb.at[zl, wp_part], t_send.at[0], t_recv.at[0],
                        at(z_=lax.rem(z + 2 * zl + NZ - 1, NZ))))
    forward(2, 1)
    forward(3, 0)
    forward(3, 1)
    for c in shares:
        c.wait_recv()
    for s in range(2):
        rows = wg[s].reshape(NZH * 8 * PAD, COLS)
        wc[0, pl.ds(s * SLICE, SLICE), :] = jnp.dot(
            pick_near[...], rows, preferred_element_type=F32).astype(BF16)

    gsend = []

    def send_g(slot, k):
        gsend.append(go(remote(gs.at[slot], gb.at[y], g_send.at[k], g_recv.at[k], at(y_=ys(k)))))

    def gradient(d):
        block = rb[2 * (d - 1):2 * d].reshape(2 * TOK, COLS)
        g = dot_nt(block, wc[0]).astype(BF16)
        gs[2 * (d - 1)] = g[:TOK]
        gs[2 * d - 1] = g[TOK:]
        send_g(2 * (d - 1), NY - d)
        send_g(2 * d - 1, d)

    gradient(1)
    gradient(2)
    far_first()
    gradient(3)
    far_second()
    loads[2].wait()
    send_wp.wait_recv()
    share_wp = go(remote(wpb.at[1 - zl, wp_part], wpb.at[1 - zl, wp_part], t_send.at[2], t_recv.at[2], sibling))

    share_wp.wait_recv()
    for s in range(2):
        dw[s] = (wc[0, pl.ds(s * SLICE, SLICE), :].astype(F32) - wpb[s].astype(F32)).astype(BF16)
    ring(0, 3, 0).wait_recv()
    ring(1, 3, 1).wait_recv()
    shard_of = [-1, 1, -2, 2, -3, 3, 0, 4]

    def scores(s, pair):
        t = dot_nt(dw[s], rb[2 * pair:2 * pair + 2].reshape(2 * TOK, COLS))
        sums = []
        for i in range(2):
            cols = pl.ds(pl.multiple_of(ys(shard_of[2 * pair + i]) * TOK, TOK), TOK)
            prod = t[:, i * TOK:(i + 1) * TOK] * tb[s, :, cols].astype(F32)
            sums.append(jnp.sum(prod, axis=0, keepdims=True))
        return sums

    loads[3].wait()
    first = [scores(zl, pair) for pair in range(4)]
    gb[y] = dot_nt(rb[OWN], wc[0]).astype(BF16)
    far_third()
    send_t.wait_recv()
    psend = []
    for pair in range(4):
        second = scores(1 - zl, pair)
        for i in range(2):
            slot, k = 2 * pair + i, shard_of[2 * pair + i] % NY
            row = jnp.broadcast_to(first[pair][i] + second[i], (8, TOK))
            if k == 0:
                sb[y] = row
            else:
                ps[slot] = row
                psend.append(go(remote(ps.at[slot], sb.at[y], p_send.at[k], p_recv.at[k], at(y_=ys(k)))))

    loads[4].wait()
    loads[5].wait()
    pos = tp * TOK + lax.broadcasted_iota(jnp.int32, (8, TOK), 1)
    start = jnp.int32(0)
    portion = jnp.zeros((8, TOK), F32)
    for k in range(8):
        n = lens[0, k]
        inside = (pos >= start) & (pos < start + n)
        frac = 1.0 / (8.0 * jnp.broadcast_to(n, (8, TOK)).astype(F32))
        portion = portion + jnp.where(inside, frac, 0.0)
        start = start + n
    base = -LOSS_MULTIPLIER * 2048.0 * portion

    far_last()
    gb[ys(4)] = dot_nt(rb[OWN], wc[1]).astype(BF16)

    for c in psend:
        c.wait_recv()
    diff = jnp.sum(sb[...], axis=0)
    coef = base * jnp.minimum(jnp.exp(diff), 1.0 + EPS_HIGH) * adv[...]
    coef = jnp.broadcast_to(coef[:1], (TOK, TOK))
    eye = ones_at(rows_of(TOK), TOK).astype(F32)
    scale = jnp.sum(jnp.where(eye > 0.0, coef, 0.0), axis=1, keepdims=True)

    for c in gsend:
        c.wait_recv()
    for i in range(NY):
        g = gb[i].astype(F32) * scale
        for s in range(2):
            out_ref[:, (s * NY + i) * SLICE:(s * NY + i + 1) * SLICE] = g[:, s * SLICE:(s + 1) * SLICE].astype(BF16)

    for c in started:
        c.wait_send()
    settle()


def local(tokens, proximal_weight, current_weight, readout, advantage, lengths):
    anywhere = pl.BlockSpec(memory_space=pl.ANY)
    dma, vmem = pltpu.SemaphoreType.DMA, pltpu.VMEM
    out = pl.pallas_call(
        kernel,
        out_shape=jax.ShapeDtypeStruct((TOK, OUT), BF16),
        in_specs=[anywhere] * 6,
        out_specs=pl.BlockSpec(memory_space=vmem),
        scratch_shapes=[
            vmem((8, TOK, COLS), BF16),
            vmem((2, SLICE, SEG), BF16),
            vmem((2, SLICE, COLS), BF16),
            vmem((2, NZH, NX, 2, PAD, COLS), BF16),
            vmem((NZ, PAD, COLS), BF16),
            vmem((NX, 2, COL, COLS), BF16),
            vmem((2, 2 * SLICE, COLS), BF16),
            vmem((2, SLICE, COLS), BF16),
            vmem((2 * SLICE, NX * 2 * COL), BF16),
            vmem((SLICE, NZH * 8 * PAD), BF16),
            vmem((6, TOK, 2 * SLICE), BF16),
            vmem((8, TOK, 2 * SLICE), BF16),
            vmem((8, 8, TOK), F32),
            vmem((8, 8, TOK), F32),
            vmem((ROWS, COLS), BF16),
            vmem((1, TOK), F32),
            pltpu.SMEM((1, 8), jnp.int32),
            dma((6,)), dma((2, 7)), dma((2, 7)), dma((2, 8)), dma((2, 8)),
            dma((4,)), dma((4,)), dma((4,)), dma((4,)),
            dma((2, 8)), dma((2, 8)), dma((8,)), dma((8,)), dma((4,)), dma((4,)),
            dma((3,)), dma((3,)), dma((8,)), dma((8,)), dma((8,)), dma((8,)), dma, dma,
        ],
        compiler_params=pltpu.CompilerParams(
            collective_id=0, has_side_effects=True, vmem_limit_bytes=VMEM_LIMIT),
        cost_estimate=pl.CostEstimate(flops=5 * 10**9, bytes_accessed=4 * 10**6, transcendentals=1024),
    )(jnp.swapaxes(tokens[0], 0, 1), proximal_weight, current_weight, readout[0], advantage, lengths)
    return out[None]


def solution(mesh):
    in_specs = (
        P("dp", None, "tp"),
        P("tp", None),
        P(("tp", "dp"), None),
        P("dp", "tp", None),
        P("dp", "tp"),
        P("dp", None),
    )
    return jax.shard_map(local, mesh=mesh, in_specs=in_specs, out_specs=P("dp", "tp", None), check_vma=False)
```

```python
import jax
import jax.numpy as jnp
from jax import lax
from jax.experimental import pallas as pl
from jax.experimental.pallas import tpu as pltpu
from jax.sharding import PartitionSpec as P

EPS_HIGH = 0.28
LOSS_MULTIPLIER = 64.0
BF16, F32 = jnp.bfloat16, jnp.float32

NX, NY, NZ, NZH = 4, 8, 8, 4
OWN, FAR = 6, 7
TOK, SEG, COLS, SLICE, OUT = 128, 1024, 1024, 320, 5120
ROWS, PAD = 10, 16
COL = NZ * ROWS
VMEM_LIMIT = 60 * 1024 * 1024


def dot_nt(a, b):
    return lax.dot_general(a, b, (((1,), (1,)), ((), ())), preferred_element_type=F32)


def tenth(v):
    return (v * 6554) >> 16


def rows_of(n):
    return lax.broadcasted_iota(jnp.int32, (n, 1), 0)


def ones_at(column, cols):
    shape = (column.shape[0], cols)
    at = jnp.broadcast_to(column, shape) == lax.broadcasted_iota(jnp.int32, shape, 1)
    return jnp.where(at, 1.0, 0.0).astype(BF16)


def kernel(tok_hbm, wp_hbm, wc_hbm, r_hbm, adv_hbm, len_hbm, out_ref,
           rb, tb, wpb, wg, wz_b, wcol, wc, dw, pick, pick_near, gs, gb, ps, sb, wc_own, adv, lens,
           loc, r_send, r_recv, wz_send, wz_recv, wx_send, wx_recv, ws_send, ws_recv, nx_send, nx_recv, ny_send, ny_recv, ns_send, ns_recv,
           t_send, t_recv, g_send, g_recv, p_send, p_recv, j_send, j_recv):
    tp, dp = lax.axis_index("tp"), lax.axis_index("dp")
    zl, y = lax.div(tp, NY), lax.rem(tp, NY)
    zh, x, core = lax.div(dp, 8), lax.rem(lax.div(dp, 2), NX), lax.rem(dp, 2)
    z = zh * 2 + zl

    def at(y_=None, x_=None, z_=None, core_=None):
        y_, x_ = y if y_ is None else y_, x if x_ is None else x_
        z_, core_ = z if z_ is None else z_, core if core_ is None else core_
        return {"tp": lax.rem(z_, 2) * NY + y_, "dp": lax.div(z_, 2) * 8 + x_ * 2 + core_}

    def ys(k):
        return lax.rem(y + (k + NY), NY)

    def xs(k):
        return lax.rem(x + (k + NX), NX)

    sibling = at(core_=1 - core)
    right, left = at(y_=ys(1)), at(y_=ys(-1))
    partner = at(z_=zh * 2 + (1 - zl))
    started = []

    def remote(src, dst, send, recv, dev):
        return pltpu.make_async_remote_copy(src_ref=src, dst_ref=dst, send_sem=send, recv_sem=recv,
                                            device_id=dev, device_id_type=pl.DeviceIdType.MESH)

    def go(copy):
        copy.start()
        started.append(copy)
        return copy

    barrier = pltpu.get_barrier_semaphore()
    peers = [at(y_=ys(k)) for k in range(1, NY)] + [at(x_=xs(1)), at(x_=xs(-1)), sibling]

    def greet(peer):
        pl.semaphore_signal(barrier, inc=1, device_id=peer, device_id_type=pl.DeviceIdType.MESH)

    for peer in peers:
        greet(peer)
    for j in range(NZ):
        @pl.when(z < j)
        def _():
            greet(at(z_=j))

    half = pl.ds(pl.multiple_of(zl * SEG, SEG), SEG)
    other = pl.ds(pl.multiple_of((1 - zl) * SEG, SEG), SEG)
    loads = [pltpu.make_async_copy(src, dst, loc.at[i]) for i, (src, dst) in enumerate((
        (wc_hbm, wc_own), (r_hbm, rb.at[OWN]), (wp_hbm, wpb.at[zl]), (tok_hbm.at[:, half], tb.at[zl]),
        (adv_hbm, adv), (len_hbm, lens)))]
    for load in loads:
        load.start()
    mine = wg.at[zl, zh, x, core]
    mine[...] = jnp.zeros((PAD, COLS), BF16)
    loads[0].wait()
    mine[pl.ds(0, ROWS), :] = wc_own[...]
    loads[1].wait()
    pl.semaphore_wait(barrier, len(peers) + z)

    def block(w, b):
        return wz_b.at[b] if w else wg.at[lax.rem(b, 2), lax.div(b, 2), x, core]

    def give(w, to):
        return remote(block(w, z), block(w, z), wz_send.at[w, to], wz_recv.at[w, z], at(z_=to))

    def came(w, b):
        remote(block(w, b), block(w, b), wz_send.at[w, b], wz_recv.at[w, b], sibling).wait_recv()

    def near_block(b, k):
        return wg.at[lax.rem(b, 2), lax.div(b, 2), xs(k), core]

    def near_over(b, i):
        src = near_block(b, 0)
        return remote(src, src, nx_send.at[i, b], nx_recv.at[i, b], at(x_=xs(-1 if i else 1)))

    def near_on(b, i):
        src = near_block(b, 1 if i else -1)
        return remote(src, src, ny_send.at[b], ny_recv.at[b], at(x_=xs(-1 if i else 1)))

    def over(b):
        for i in range(2):
            near_over(b, i).start()

    def lower():
        for k in range(1, NZ):
            @pl.when(k <= z)
            def _():
                give(0, z - k).start()

    def higher(*steps):
        for k in steps:
            @pl.when(z + k < NZ)
            def _():
                came(0, z + k)
                give(0, z + k).start()
                over(z + k)

    def from_lower():
        for k in range(1, NZ):
            @pl.when(k <= z)
            def _():
                came(0, z - k)
                over(z - k)

    def onward(b):
        for i in range(2):
            src = near_block(b, 1 if i else -1)
            remote(src, src, nx_send.at[i, b], nx_recv.at[i, b], sibling).wait_recv()
        for i in range(2):
            @pl.when(lax.rem(b, 2) == i)
            def _():
                near_on(b, i).start()

    def onward_lower():
        for k in range(NZ):
            @pl.when(k <= z)
            def _():
                onward(z - k)

    def onward_higher():
        for k in range(1, NZ):
            @pl.when(z + k < NZ)
            def _():
                onward(z + k)

    def near_column(k):
        return wg.at[:, :, xs(k), core]

    def near_share(k):
        c = remote(near_column(k), near_column(k), ns_send.at[k % NX], ns_recv.at[k % NX], sibling)
        return go(c)

    def gathered():
        for b in range(NZ):
            @pl.when(b != z)
            def _():
                came(1, b)

    def settle():
        for b in range(NZ):
            @pl.when(b != z)
            def _():
                give(0, b).wait_send()
            for i in range(2):
                near_over(b, i).wait_send()
            near_on(b, b % 2).wait_send()

    lower()
    over(z)

    def chunk(slot, h):
        return rb.at[slot, pl.ds(h * (TOK // 2), TOK // 2)]

    def slot_of(side, d):
        return OWN if d == 0 else FAR if d == 4 else 2 * (d - 1) + side

    def ring(side, d, h):
        i = 2 * d + h if d < 3 else 6
        return remote(chunk(slot_of(side, d), h), chunk(slot_of(side, d + 1), h),
                      r_send.at[side, i], r_recv.at[side, i], left if side else right)

    go(ring(0, 0, 0))
    go(ring(1, 0, 0))
    jump = go(remote(mine, wz_b.at[z], j_send, j_recv, at(y_=ys(4))))
    go(ring(0, 0, 1))
    go(ring(1, 0, 1))

    def forward(d, h):
        for side in range(2):
            ring(side, d - 1, h).wait_recv()
            if d < 3 or h == side:
                go(ring(side, d, h))

    t_i = rows_of(COL)
    t_b = tenth(t_i)
    pick_col = ones_at((2 * (t_b & (NZH - 1)) + (t_b >> 2)) * PAD + t_i - t_b * ROWS, NZ * PAD)
    r_i = rows_of(2 * SLICE)
    r_s = jnp.where(r_i >= SLICE, 1, 0)
    r_f = r_i - r_s * SLICE
    r_b = tenth(r_f)
    q_i = rows_of(SLICE)
    q_b = tenth(q_i)
    pick_near[...] = ones_at(q_b * PAD + q_i - q_b * ROWS, NZH * 8 * PAD)
    pick[...] = ones_at((r_b & 7) * COL + (r_s * NZH + (r_b >> 3)) * ROWS + r_f - r_b * ROWS, NX * 2 * COL)

    higher(1, 2)
    forward(1, 0)
    higher(3, 4)
    from_lower()
    higher(5, 6, 7)
    jump.wait_recv()
    for k in range(1, NZ):
        go(give(1, lax.rem(z + k, NZ)))
    onward_lower()
    forward(1, 1)
    shares = [near_share(0)]
    onward_higher()
    shares += [near_share(1), near_share(-1)]
    forward(2, 0)

    def column(k, part=None):
        ref = wcol.at[xs(k), core]
        return ref if part is None else ref.at[pl.ds(*part)]

    def far_over(i, k, src):
        return go(remote(src, src, wx_send.at[i], wx_recv.at[i], at(x_=xs(k))))

    far_own, far_shares = [], []

    def far_share(k):
        far_shares.append(go(remote(column(k), column(k), ws_send.at[k % NX], ws_recv.at[k % NX], sibling)))

    def far_first():
        gathered()
        wcol[x, core] = jnp.dot(
            pick_col, wz_b[...].reshape(NZ * PAD, COLS), preferred_element_type=F32).astype(BF16)
        far_own.extend(far_over(i, k, column(0)) for i, k in enumerate((1, -1)))
        far_share(0)

    def far_second():
        for i, (k, part) in enumerate(((1, (0, 48)), (-1, (48, 32)))):
            far_own[i].wait_recv()
            far_own.append(far_over(2 + i, k, column(-k, part)))
            far_share(-k)

    def far_third():
        far_own[2].wait_recv()
        far_own[3].wait_recv()
        far_share(2)

    def far_last():
        for c in far_shares:
            c.wait_recv()
        wc[1] = jnp.dot(
            pick[...], wcol[...].reshape(NX * 2 * COL, COLS), preferred_element_type=F32).astype(BF16)

    for b in range(NZ):
        near_on(b, b % 2).wait_recv()
    shares.append(near_share(2))
    send_t = go(remote(tok_hbm.at[:, other], tb.at[zl], t_send.at[1], t_recv.at[1], partner))
    wp_part = pl.ds(pl.multiple_of(core * (SLICE // 2), SLICE // 2), SLICE // 2)
    send_wp = go(remote(wp_hbm.at[wp_part], wpb.at[zl, wp_part], t_send.at[0], t_recv.at[0],
                        at(z_=lax.rem(z + 2 * zl + NZ - 1, NZ))))
    forward(2, 1)
    forward(3, 0)
    forward(3, 1)
    far_first()
    for c in shares:
        c.wait_recv()
    for s in range(2):
        rows = wg[s].reshape(NZH * 8 * PAD, COLS)
        wc[0, pl.ds(s * SLICE, SLICE), :] = jnp.dot(
            pick_near[...], rows, preferred_element_type=F32).astype(BF16)

    gsend = []

    def send_g(slot, k):
        gsend.append(go(remote(gs.at[slot], gb.at[y], g_send.at[k], g_recv.at[k], at(y_=ys(k)))))

    def gradient(d):
        block = rb[2 * (d - 1):2 * d].reshape(2 * TOK, COLS)
        g = dot_nt(block, wc[0]).astype(BF16)
        gs[2 * (d - 1)] = g[:TOK]
        gs[2 * d - 1] = g[TOK:]
        send_g(2 * (d - 1), NY - d)
        send_g(2 * d - 1, d)

    gradient(1)
    gradient(2)
    gradient(3)
    far_second()
    loads[2].wait()
    send_wp.wait_recv()
    share_wp = go(remote(wpb.at[1 - zl, wp_part], wpb.at[1 - zl, wp_part], t_send.at[2], t_recv.at[2], sibling))

    share_wp.wait_recv()
    for s in range(2):
        dw[s] = (wc[0, pl.ds(s * SLICE, SLICE), :].astype(F32) - wpb[s].astype(F32)).astype(BF16)
    ring(0, 3, 0).wait_recv()
    ring(1, 3, 1).wait_recv()
    shard_of = [-1, 1, -2, 2, -3, 3, 0, 4]

    def scores(s, pair):
        t = dot_nt(dw[s], rb[2 * pair:2 * pair + 2].reshape(2 * TOK, COLS))
        sums = []
        for i in range(2):
            cols = pl.ds(pl.multiple_of(ys(shard_of[2 * pair + i]) * TOK, TOK), TOK)
            prod = t[:, i * TOK:(i + 1) * TOK] * tb[s, :, cols].astype(F32)
            sums.append(jnp.sum(prod, axis=0, keepdims=True))
        return sums

    loads[3].wait()
    first = [scores(zl, pair) for pair in range(4)]
    gb[y] = dot_nt(rb[OWN], wc[0]).astype(BF16)
    far_third()
    send_t.wait_recv()
    psend = []
    for pair in range(4):
        second = scores(1 - zl, pair)
        for i in range(2):
            slot, k = 2 * pair + i, shard_of[2 * pair + i] % NY
            row = jnp.broadcast_to(first[pair][i] + second[i], (8, TOK))
            if k == 0:
                sb[y] = row
            else:
                ps[slot] = row
                psend.append(go(remote(ps.at[slot], sb.at[y], p_send.at[k], p_recv.at[k], at(y_=ys(k)))))

    loads[4].wait()
    loads[5].wait()
    pos = tp * TOK + lax.broadcasted_iota(jnp.int32, (8, TOK), 1)
    start = jnp.int32(0)
    portion = jnp.zeros((8, TOK), F32)
    for k in range(8):
        n = lens[0, k]
        inside = (pos >= start) & (pos < start + n)
        frac = 1.0 / (8.0 * jnp.broadcast_to(n, (8, TOK)).astype(F32))
        portion = portion + jnp.where(inside, frac, 0.0)
        start = start + n
    base = -LOSS_MULTIPLIER * 2048.0 * portion

    far_last()
    gb[ys(4)] = dot_nt(rb[OWN], wc[1]).astype(BF16)

    for c in psend:
        c.wait_recv()
    diff = jnp.sum(sb[...], axis=0)
    coef = base * jnp.minimum(jnp.exp(diff), 1.0 + EPS_HIGH) * adv[...]
    coef = jnp.broadcast_to(coef[:1], (TOK, TOK))
    eye = ones_at(rows_of(TOK), TOK).astype(F32)
    scale = jnp.sum(jnp.where(eye > 0.0, coef, 0.0), axis=1, keepdims=True)

    settle()
    for c in started:
        if all(c is not g for g in gsend):
            c.wait_send()
    for c in gsend:
        c.wait_recv()
    for i in range(NY):
        g = gb[i].astype(F32) * scale
        for s in range(2):
            out_ref[:, (s * NY + i) * SLICE:(s * NY + i + 1) * SLICE] = g[:, s * SLICE:(s + 1) * SLICE].astype(BF16)

    for c in gsend:
        c.wait_send()


def local(tokens, proximal_weight, current_weight, readout, advantage, lengths):
    anywhere = pl.BlockSpec(memory_space=pl.ANY)
    dma, vmem = pltpu.SemaphoreType.DMA, pltpu.VMEM
    out = pl.pallas_call(
        kernel,
        out_shape=jax.ShapeDtypeStruct((TOK, OUT), BF16),
        in_specs=[anywhere] * 6,
        out_specs=pl.BlockSpec(memory_space=vmem),
        scratch_shapes=[
            vmem((8, TOK, COLS), BF16),
            vmem((2, SLICE, SEG), BF16),
            vmem((2, SLICE, COLS), BF16),
            vmem((2, NZH, NX, 2, PAD, COLS), BF16),
            vmem((NZ, PAD, COLS), BF16),
            vmem((NX, 2, COL, COLS), BF16),
            vmem((2, 2 * SLICE, COLS), BF16),
            vmem((2, SLICE, COLS), BF16),
            vmem((2 * SLICE, NX * 2 * COL), BF16),
            vmem((SLICE, NZH * 8 * PAD), BF16),
            vmem((6, TOK, 2 * SLICE), BF16),
            vmem((8, TOK, 2 * SLICE), BF16),
            vmem((8, 8, TOK), F32),
            vmem((8, 8, TOK), F32),
            vmem((ROWS, COLS), BF16),
            vmem((1, TOK), F32),
            pltpu.SMEM((1, 8), jnp.int32),
            dma((6,)), dma((2, 7)), dma((2, 7)), dma((2, 8)), dma((2, 8)),
            dma((4,)), dma((4,)), dma((4,)), dma((4,)),
            dma((2, 8)), dma((2, 8)), dma((8,)), dma((8,)), dma((4,)), dma((4,)),
            dma((3,)), dma((3,)), dma((8,)), dma((8,)), dma((8,)), dma((8,)), dma, dma,
        ],
        compiler_params=pltpu.CompilerParams(
            collective_id=0, has_side_effects=True, vmem_limit_bytes=VMEM_LIMIT),
        cost_estimate=pl.CostEstimate(flops=5 * 10**9, bytes_accessed=4 * 10**6, transcendentals=1024),
    )(jnp.swapaxes(tokens[0], 0, 1), proximal_weight, current_weight, readout[0], advantage, lengths)
    return out[None]


def solution(mesh):
    in_specs = (
        P("dp", None, "tp"),
        P("tp", None),
        P(("tp", "dp"), None),
        P("dp", "tp", None),
        P("dp", "tp"),
        P("dp", None),
    )
    return jax.shard_map(local, mesh=mesh, in_specs=in_specs, out_specs=P("dp", "tp", None), check_vma=False)
```

```python
import jax
import jax.numpy as jnp
from jax import lax
from jax.experimental import pallas as pl
from jax.experimental.pallas import tpu as pltpu
from jax.sharding import PartitionSpec as P

EPS_HIGH = 0.28
LOSS_MULTIPLIER = 64.0
BF16, F32 = jnp.bfloat16, jnp.float32

NX, NY, NZ, NZH = 4, 8, 8, 4
OWN, FAR = 6, 7
TOK, SEG, COLS, SLICE, OUT = 128, 1024, 1024, 320, 5120
ROWS, PAD = 10, 16
COL = NZ * ROWS
VMEM_LIMIT = 60 * 1024 * 1024


def dot_nt(a, b):
    return lax.dot_general(a, b, (((1,), (1,)), ((), ())), preferred_element_type=F32)


def tenth(v):
    return (v * 6554) >> 16


def rows_of(n):
    return lax.broadcasted_iota(jnp.int32, (n, 1), 0)


def ones_at(column, cols):
    shape = (column.shape[0], cols)
    at = jnp.broadcast_to(column, shape) == lax.broadcasted_iota(jnp.int32, shape, 1)
    return jnp.where(at, 1.0, 0.0).astype(BF16)


def kernel(tok_hbm, wp_hbm, wc_hbm, r_hbm, adv_hbm, len_hbm, out_ref,
           rb, tb, wpb, wg, wz_b, wcol, wc, dw, pick, pick_near, gs, gb, ps, sb, adv, lens,
           loc, r_send, r_recv, wz_send, wz_recv, wx_send, wx_recv, ws_send, ws_recv, nx_send, nx_recv, ny_send, ny_recv, ns_send, ns_recv,
           t_send, t_recv, g_send, g_recv, p_send, p_recv, j_send, j_recv):
    tp, dp = lax.axis_index("tp"), lax.axis_index("dp")
    zl, y = lax.div(tp, NY), lax.rem(tp, NY)
    zh, x, core = lax.div(dp, 8), lax.rem(lax.div(dp, 2), NX), lax.rem(dp, 2)
    z = zh * 2 + zl

    def at(y_=None, x_=None, z_=None, core_=None):
        y_, x_ = y if y_ is None else y_, x if x_ is None else x_
        z_, core_ = z if z_ is None else z_, core if core_ is None else core_
        return {"tp": lax.rem(z_, 2) * NY + y_, "dp": lax.div(z_, 2) * 8 + x_ * 2 + core_}

    def ys(k):
        return lax.rem(y + (k + NY), NY)

    def xs(k):
        return lax.rem(x + (k + NX), NX)

    sibling = at(core_=1 - core)
    right, left = at(y_=ys(1)), at(y_=ys(-1))
    partner = at(z_=zh * 2 + (1 - zl))
    started = []

    def remote(src, dst, send, recv, dev):
        return pltpu.make_async_remote_copy(src_ref=src, dst_ref=dst, send_sem=send, recv_sem=recv,
                                            device_id=dev, device_id_type=pl.DeviceIdType.MESH)

    def go(copy):
        copy.start()
        started.append(copy)
        return copy

    barrier = pltpu.get_barrier_semaphore()
    peers = [at(y_=ys(k)) for k in range(1, NY)] + [at(x_=xs(1)), at(x_=xs(-1)), sibling]

    def greet(peer):
        pl.semaphore_signal(barrier, inc=1, device_id=peer, device_id_type=pl.DeviceIdType.MESH)

    for peer in peers:
        greet(peer)
    for j in range(NZ):
        @pl.when(z < j)
        def _():
            greet(at(z_=j))

    half = pl.ds(pl.multiple_of(zl * SEG, SEG), SEG)
    other = pl.ds(pl.multiple_of((1 - zl) * SEG, SEG), SEG)
    mine = wg.at[zl, zh, x, core]
    loads = [pltpu.make_async_copy(src, dst, loc.at[i]) for i, (src, dst) in enumerate((
        (wc_hbm, mine), (r_hbm, rb.at[OWN]), (wp_hbm, wpb.at[zl]), (tok_hbm.at[:, half], tb.at[zl]),
        (adv_hbm, adv), (len_hbm, lens)))]
    for load in loads:
        load.start()
    loads[0].wait()
    loads[1].wait()
    pl.semaphore_wait(barrier, len(peers) + z)

    def block(w, b):
        return wz_b.at[b] if w else wg.at[lax.rem(b, 2), lax.div(b, 2), x, core]

    def give(w, to):
        return remote(block(w, z), block(w, z), wz_send.at[w, to], wz_recv.at[w, z], at(z_=to))

    def came(w, b):
        remote(block(w, b), block(w, b), wz_send.at[w, b], wz_recv.at[w, b], sibling).wait_recv()

    def near_block(b, k):
        return wg.at[lax.rem(b, 2), lax.div(b, 2), xs(k), core]

    def near_over(b, i):
        src = near_block(b, 0)
        return remote(src, src, nx_send.at[i, b], nx_recv.at[i, b], at(x_=xs(-1 if i else 1)))

    def near_on(b, i):
        src = near_block(b, 1 if i else -1)
        return remote(src, src, ny_send.at[b], ny_recv.at[b], at(x_=xs(-1 if i else 1)))

    def over(b):
        for i in range(2):
            near_over(b, i).start()

    def lower():
        for k in range(1, NZ):
            @pl.when(k <= z)
            def _():
                give(0, z - k).start()

    def higher(*steps):
        for k in steps:
            @pl.when(z + k < NZ)
            def _():
                came(0, z + k)
                give(0, z + k).start()
                over(z + k)

    def from_lower():
        for k in range(1, NZ):
            @pl.when(k <= z)
            def _():
                came(0, z - k)
                over(z - k)

    def onward(b):
        for i in range(2):
            src = near_block(b, 1 if i else -1)
            remote(src, src, nx_send.at[i, b], nx_recv.at[i, b], sibling).wait_recv()
        for i in range(2):
            @pl.when(lax.rem(b, 2) == i)
            def _():
                near_on(b, i).start()

    def onward_lower():
        for k in range(NZ):
            @pl.when(k <= z)
            def _():
                onward(z - k)

    def onward_higher():
        for k in range(1, NZ):
            @pl.when(z + k < NZ)
            def _():
                onward(z + k)

    def near_column(k):
        return wg.at[:, :, xs(k), core]

    def near_share(k):
        c = remote(near_column(k), near_column(k), ns_send.at[k % NX], ns_recv.at[k % NX], sibling)
        return go(c)

    def gathered():
        for b in range(NZ):
            @pl.when(b != z)
            def _():
                came(1, b)

    def settle():
        for b in range(NZ):
            @pl.when(b != z)
            def _():
                give(0, b).wait_send()
            for i in range(2):
                near_over(b, i).wait_send()
            near_on(b, b % 2).wait_send()

    lower()
    over(z)

    def chunk(slot, h):
        return rb.at[slot, pl.ds(h * (TOK // 2), TOK // 2)]

    def slot_of(side, d):
        return OWN if d == 0 else FAR if d == 4 else 2 * (d - 1) + side

    def ring(side, d, h):
        i = 2 * d + h if d < 3 else 6
        return remote(chunk(slot_of(side, d), h), chunk(slot_of(side, d + 1), h),
                      r_send.at[side, i], r_recv.at[side, i], left if side else right)

    go(ring(0, 0, 0))
    go(ring(1, 0, 0))
    jump = go(remote(mine, wz_b.at[z], j_send, j_recv, at(y_=ys(4))))
    go(ring(0, 0, 1))
    go(ring(1, 0, 1))

    def forward(d, h):
        for side in range(2):
            ring(side, d - 1, h).wait_recv()
            if d < 3 or h == side:
                go(ring(side, d, h))

    t_i = rows_of(COL)
    t_b = tenth(t_i)
    pick_col = ones_at((2 * (t_b & (NZH - 1)) + (t_b >> 2)) * PAD + t_i - t_b * ROWS, NZ * PAD)
    r_i = rows_of(2 * SLICE)
    r_s = jnp.where(r_i >= SLICE, 1, 0)
    r_f = r_i - r_s * SLICE
    r_b = tenth(r_f)
    q_i = rows_of(SLICE)
    q_b = tenth(q_i)
    pick_near[...] = ones_at(q_b * PAD + q_i - q_b * ROWS, NZH * 8 * PAD)
    pick[...] = ones_at((r_b & 7) * COL + (r_s * NZH + (r_b >> 3)) * ROWS + r_f - r_b * ROWS, NX * 2 * COL)

    higher(1, 2)
    forward(1, 0)
    higher(3, 4)
    from_lower()
    higher(5, 6, 7)
    jump.wait_recv()
    for k in range(1, NZ):
        go(give(1, lax.rem(z + k, NZ)))
    onward_lower()
    forward(1, 1)
    shares = [near_share(0)]
    onward_higher()
    shares += [near_share(1), near_share(-1)]
    forward(2, 0)

    def column(k, part=None):
        ref = wcol.at[xs(k), core]
        return ref if part is None else ref.at[pl.ds(*part)]

    def far_over(i, k, src):
        return go(remote(src, src, wx_send.at[i], wx_recv.at[i], at(x_=xs(k))))

    far_own, far_shares = [], []

    def far_share(k):
        far_shares.append(go(remote(column(k), column(k), ws_send.at[k % NX], ws_recv.at[k % NX], sibling)))

    def far_first():
        gathered()
        wcol[x, core] = jnp.dot(
            pick_col, wz_b[...].reshape(NZ * PAD, COLS), preferred_element_type=F32).astype(BF16)
        far_own.extend(far_over(i, k, column(0)) for i, k in enumerate((1, -1)))
        far_share(0)

    def far_second():
        for i, (k, part) in enumerate(((1, (0, 48)), (-1, (48, 32)))):
            far_own[i].wait_recv()
            far_own.append(far_over(2 + i, k, column(-k, part)))
            far_share(-k)

    def far_third():
        far_own[2].wait_recv()
        far_own[3].wait_recv()
        far_share(2)

    def far_last():
        for c in far_shares:
            c.wait_recv()
        wc[1] = jnp.dot(
            pick[...], wcol[...].reshape(NX * 2 * COL, COLS), preferred_element_type=F32).astype(BF16)

    for b in range(NZ):
        near_on(b, b % 2).wait_recv()
    shares.append(near_share(2))
    send_t = go(remote(tok_hbm.at[:, other], tb.at[zl], t_send.at[1], t_recv.at[1], partner))
    wp_part = pl.ds(pl.multiple_of(core * (SLICE // 2), SLICE // 2), SLICE // 2)
    send_wp = go(remote(wp_hbm.at[wp_part], wpb.at[zl, wp_part], t_send.at[0], t_recv.at[0],
                        at(z_=lax.rem(z + 2 * zl + NZ - 1, NZ))))
    forward(2, 1)
    forward(3, 0)
    forward(3, 1)
    far_first()
    for c in shares:
        c.wait_recv()
    for s in range(2):
        rows = wg[s].reshape(NZH * 8 * PAD, COLS)
        wc[0, pl.ds(s * SLICE, SLICE), :] = jnp.dot(
            pick_near[...], rows, preferred_element_type=F32).astype(BF16)

    gsend = []

    def send_g(slot, k):
        gsend.append(go(remote(gs.at[slot], gb.at[y], g_send.at[k], g_recv.at[k], at(y_=ys(k)))))

    def gradient(d):
        block = rb[2 * (d - 1):2 * d].reshape(2 * TOK, COLS)
        g = dot_nt(block, wc[0]).astype(BF16)
        gs[2 * (d - 1)] = g[:TOK]
        gs[2 * d - 1] = g[TOK:]
        send_g(2 * (d - 1), NY - d)
        send_g(2 * d - 1, d)

    gradient(1)
    gradient(2)
    gradient(3)
    far_second()
    loads[2].wait()
    send_wp.wait_recv()
    share_wp = go(remote(wpb.at[1 - zl, wp_part], wpb.at[1 - zl, wp_part], t_send.at[2], t_recv.at[2], sibling))

    share_wp.wait_recv()
    for s in range(2):
        dw[s] = (wc[0, pl.ds(s * SLICE, SLICE), :].astype(F32) - wpb[s].astype(F32)).astype(BF16)
    ring(0, 3, 0).wait_recv()
    ring(1, 3, 1).wait_recv()
    shard_of = [-1, 1, -2, 2, -3, 3, 0, 4]

    def scores(s, pair):
        t = dot_nt(dw[s], rb[2 * pair:2 * pair + 2].reshape(2 * TOK, COLS))
        sums = []
        for i in range(2):
            cols = pl.ds(pl.multiple_of(ys(shard_of[2 * pair + i]) * TOK, TOK), TOK)
            prod = t[:, i * TOK:(i + 1) * TOK] * tb[s, :, cols].astype(F32)
            sums.append(jnp.sum(prod, axis=0, keepdims=True))
        return sums

    loads[3].wait()
    first = [scores(zl, pair) for pair in range(4)]
    gb[y] = dot_nt(rb[OWN], wc[0]).astype(BF16)
    far_third()
    send_t.wait_recv()
    psend = []
    for pair in range(4):
        second = scores(1 - zl, pair)
        for i in range(2):
            slot, k = 2 * pair + i, shard_of[2 * pair + i] % NY
            row = jnp.broadcast_to(first[pair][i] + second[i], (8, TOK))
            if k == 0:
                sb[y] = row
            else:
                ps[slot] = row
                psend.append(go(remote(ps.at[slot], sb.at[y], p_send.at[k], p_recv.at[k], at(y_=ys(k)))))

    loads[4].wait()
    loads[5].wait()
    pos = tp * TOK + lax.broadcasted_iota(jnp.int32, (8, TOK), 1)
    start = jnp.int32(0)
    portion = jnp.zeros((8, TOK), F32)
    for k in range(8):
        n = lens[0, k]
        inside = (pos >= start) & (pos < start + n)
        frac = 1.0 / (8.0 * jnp.broadcast_to(n, (8, TOK)).astype(F32))
        portion = portion + jnp.where(inside, frac, 0.0)
        start = start + n
    base = -LOSS_MULTIPLIER * 2048.0 * portion

    far_last()
    gb[ys(4)] = dot_nt(rb[OWN], wc[1]).astype(BF16)

    for c in psend:
        c.wait_recv()
    diff = jnp.sum(sb[...], axis=0)
    coef = base * jnp.minimum(jnp.exp(diff), 1.0 + EPS_HIGH) * adv[...]
    coef = jnp.broadcast_to(coef[:1], (TOK, TOK))
    eye = ones_at(rows_of(TOK), TOK).astype(F32)
    scale = jnp.sum(jnp.where(eye > 0.0, coef, 0.0), axis=1, keepdims=True)

    settle()
    for c in started:
        if all(c is not g for g in gsend):
            c.wait_send()
    for c in gsend:
        c.wait_recv()
    for i in range(NY):
        g = gb[i].astype(F32) * scale
        for s in range(2):
            out_ref[:, (s * NY + i) * SLICE:(s * NY + i + 1) * SLICE] = g[:, s * SLICE:(s + 1) * SLICE].astype(BF16)

    for c in gsend:
        c.wait_send()


def local(tokens, proximal_weight, current_weight, readout, advantage, lengths):
    anywhere = pl.BlockSpec(memory_space=pl.ANY)
    dma, vmem = pltpu.SemaphoreType.DMA, pltpu.VMEM
    out = pl.pallas_call(
        kernel,
        out_shape=jax.ShapeDtypeStruct((TOK, OUT), BF16),
        in_specs=[anywhere] * 6,
        out_specs=pl.BlockSpec(memory_space=vmem),
        scratch_shapes=[
            vmem((8, TOK, COLS), BF16),
            vmem((2, SLICE, SEG), BF16),
            vmem((2, SLICE, COLS), BF16),
            vmem((2, NZH, NX, 2, PAD, COLS), BF16),
            vmem((NZ, PAD, COLS), BF16),
            vmem((NX, 2, COL, COLS), BF16),
            vmem((2, 2 * SLICE, COLS), BF16),
            vmem((2, SLICE, COLS), BF16),
            vmem((2 * SLICE, NX * 2 * COL), BF16),
            vmem((SLICE, NZH * 8 * PAD), BF16),
            vmem((6, TOK, 2 * SLICE), BF16),
            vmem((8, TOK, 2 * SLICE), BF16),
            vmem((8, 8, TOK), F32),
            vmem((8, 8, TOK), F32),
            vmem((1, TOK), F32),
            pltpu.SMEM((1, 8), jnp.int32),
            dma((6,)), dma((2, 7)), dma((2, 7)), dma((2, 8)), dma((2, 8)),
            dma((4,)), dma((4,)), dma((4,)), dma((4,)),
            dma((2, 8)), dma((2, 8)), dma((8,)), dma((8,)), dma((4,)), dma((4,)),
            dma((3,)), dma((3,)), dma((8,)), dma((8,)), dma((8,)), dma((8,)), dma, dma,
        ],
        compiler_params=pltpu.CompilerParams(
            collective_id=0, has_side_effects=True, vmem_limit_bytes=VMEM_LIMIT),
        cost_estimate=pl.CostEstimate(flops=5 * 10**9, bytes_accessed=4 * 10**6, transcendentals=1024),
    )(jnp.swapaxes(tokens[0], 0, 1), proximal_weight, jnp.pad(current_weight, ((0, PAD - ROWS), (0, 0))),
      readout[0], advantage, lengths)
    return out[None]


def solution(mesh):
    in_specs = (
        P("dp", None, "tp"),
        P("tp", None),
        P(("tp", "dp"), None),
        P("dp", "tp", None),
        P("dp", "tp"),
        P("dp", None),
    )
    return jax.shard_map(local, mesh=mesh, in_specs=in_specs, out_specs=P("dp", "tp", None), check_vma=False)
```
